32 devices in a mesh: row: 8 (over z, y), col: 4 (over x, core).
Axes of the slice: x: 2, y: 2, z: 4, core: 2. Of those that a mesh axis runs over, the one named last changes fastest.
Arguments:
- hidden: bfloat16 [4096, 1152], P('row', 'col'), may hold values from -60 to 60
- noisy_latent: bfloat16 [512, 128], P('row'), may hold values from -6 to 6
- tile_latent: int32 [32], replicated, may hold values from 0 to 14, as said below
- timesteps: int32 [32], replicated, may hold values from 0 to 49
- step_embedding: bfloat16 [50, 1152], replicated, may hold values from -6 to 6
- alpha_now: float32 [50], replicated, may hold values from 0.25 to 0.95
- alpha_next: float32 [50], replicated, may hold values from 0.3 to 0.99
- modulation: bfloat16 [1152, 8, 1152], P('row', None, 'col'), may hold values from -0.1875 to 0.1875
- attention_in: bfloat16 [1152, 3, 1152], P(None, None, 'col'), may hold values from -6 to 6
- attention_out: bfloat16 [1152, 1152], P('col'), may hold values from -0.1875 to 0.1875
- expand_weight: bfloat16 [1152, 2304], P('row', 'col'), may hold values from -0.1875 to 0.1875
- reduce_weight: bfloat16 [2304, 1152], P('col', 'row'), may hold values from -0.125 to 0.125
- noise_head: bfloat16 [1152, 16], P('col'), may hold values from -0.1875 to 0.1875
- preview_kernel: float32 [3, 3, 4, 4], replicated, may hold values from -1 to 1
Outputs:
- stepped: bfloat16 [512, 128], P('row')
- preview: bfloat16 [512, 128], P('row')
The draws below stay inside these ranges and needn't reach their ends.
Inputs may be any that keep to these rules, and one draw needn't show every extreme that they name: `tile_latent`: latent ids start at 0 on the first tile and rise by 0 or 1 from one tile to the next; the first 4 tiles form latent 0, and every later aligned group of 4 tiles holds exactly two latents of 1 to 3 consecutive tiles each.
All inputs are finite; a program needn't handle non-finite values.
Results may differ from the reference program's by a relative error of at most 0.015.
Values may be sent and summed in bfloat16 or wider, within the bound.
No kernel may reach another device: no remote copies, remote signals or barrier semaphores. Data moves between devices by JAX's collectives and lax.ppermute only.
A program may use at most 64 MiB of HBM per device.

```python
import jax
import jax.numpy as jnp
from jax import lax

D = 1152
HEADS = 16
HEAD_DIM = 72
PATCH = 2
CHANNELS = 4
FF = 2304
GRIDW = 16
TILE_ROWS = 8
MAXT = 4
STEPS = 50
TILE = 128
TILES_ALL = 32
TOKENS = 4096
NLAT = 32
LROWS = 512
LWIDTH = 128
NOISE = 16
N_COL = 4


def draw_hidden(key, part):
    base_key = jax.random.fold_in(jax.random.fold_in(key, 11), 0)
    base_rows = jnp.clip(jax.random.normal(base_key, (TOKENS, D), jnp.float32), -6.0, 6.0)
    return base_rows.astype(jnp.bfloat16)


def draw_attention_in(key, part):
    base_key = jax.random.fold_in(jax.random.fold_in(key, 23), 0)
    weights = jnp.clip(jax.random.normal(base_key, (D, 3, D), jnp.float32), -6.0, 6.0) * D ** (-0.5)
    return jnp.clip(weights, -6.0, 6.0).astype(jnp.bfloat16)


def draw_tile_latent(key, part):
    split_key = jax.random.fold_in(key, 37)
    groups = TILES_ALL // MAXT
    index = jnp.arange(TILES_ALL, dtype=jnp.int32)
    split_at = jax.random.randint(split_key, (groups,), 1, MAXT, jnp.int32)
    within = index % MAXT
    group_of = index // MAXT
    split_here = jnp.repeat(split_at, MAXT)
    breaks = jnp.where((within == 0) | (within == split_here), 1, 0)
    breaks = jnp.where(group_of == 0, 0, breaks)
    return jnp.cumsum(breaks).astype(jnp.int32)


def with_ends(result, own_key, smallest, largest):
    place = [jax.random.randint(jax.random.fold_in(own_key, axis), (), 0, length) for axis, length in enumerate(result.shape)]
    main_axis = result.shape.index(max(result.shape))
    neighbour = place[:main_axis] + [(place[main_axis] + 1) % result.shape[main_axis]] + place[main_axis + 1:]
    return result.at[tuple(place)].set(smallest).at[tuple(neighbour)].set(largest)


def levels(key, dims, cuts, least, top_value):
    factor_of, own = 1.0, jax.random.fold_in(key, 6)
    for dim, parts in cuts:
        heights = jnp.exp(jax.random.uniform(jax.random.fold_in(own, dim), (parts,), jnp.float32, least / len(cuts), top_value / len(cuts)))
        factor_of = factor_of * jnp.repeat(heights, dims[dim] // parts).reshape([-1 if axis == dim else 1 for axis in range(len(dims))])
    return factor_of


def bell_draw(rng, extent, deviation, reach, cuts=(), held_as=jnp.bfloat16):
    array = deviation * jax.random.normal(rng, extent, jnp.float32)
    if cuts:
        array = array * levels(rng, extent, cuts, -0.22, 0.18)
    return jnp.clip(array, -reach, reach).astype(held_as)


def setup_inputs(seed: int = 0) -> dict:
    key_of = jax.random.split(jax.random.key(seed), 15)
    hidden = draw_hidden(jax.random.fold_in(key_of[14], 71), 0)
    noisy_latent = bell_draw(key_of[1], (LROWS, LWIDTH), 1.0, 6.0, ((0, 8),))
    tile_latent = draw_tile_latent(jax.random.fold_in(key_of[14], 71), 0)
    timesteps = with_ends(jax.random.randint(key_of[3], (NLAT,), 0, STEPS), jax.random.fold_in(key_of[3], 1), 0, STEPS - 1).astype(jnp.int32)
    step_embedding = bell_draw(key_of[4], (STEPS, D), 1.0, 6.0)
    alpha_now = jnp.clip(jax.random.uniform(key_of[5], (STEPS,), jnp.float32, 0.25, 0.95), 0.25, 0.95)
    alpha_next = jnp.clip(jax.random.uniform(key_of[6], (STEPS,), jnp.float32, 0.3, 0.99), 0.3, 0.99)
    modulation = bell_draw(key_of[7], (D, 8, D), D ** -0.5, 0.1875, ((0, 8), (2, 4)))
    attention_in = draw_attention_in(jax.random.fold_in(key_of[14], 71), 0)
    attention_out = bell_draw(key_of[9], (D, D), D ** -0.5, 0.1875, ((0, 4),))
    expand_weight = bell_draw(key_of[10], (D, FF), D ** -0.5, 0.1875, ((0, 8), (1, 4)))
    reduce_weight = bell_draw(key_of[11], (FF, D), FF ** -0.5, 0.125, ((0, 4), (1, 8)))
    noise_head = bell_draw(key_of[12], (D, NOISE), D ** -0.5, 0.1875, ((0, 4),))
    preview_kernel = bell_draw(key_of[13], (3, 3, CHANNELS, CHANNELS), (9 * CHANNELS) ** -0.5, 1.0, (), jnp.float32)
    return {"hidden": hidden, "noisy_latent": noisy_latent, "tile_latent": tile_latent, "timesteps": timesteps, "step_embedding": step_embedding, "alpha_now": alpha_now, "alpha_next": alpha_next, "modulation": modulation, "attention_in": attention_in, "attention_out": attention_out, "expand_weight": expand_weight, "reduce_weight": reduce_weight, "noise_head": noise_head, "preview_kernel": preview_kernel}


EPS_NORM = 1e-06

def modulate_tiles(values, shift_term, scale_term):
    mean_value = lax.optimization_barrier(jnp.sum(values, axis=-1, keepdims=True)) / D
    spread = lax.optimization_barrier(jnp.sum(values * values, axis=-1, keepdims=True)) / D - mean_value * mean_value
    normed = (values - mean_value) * lax.rsqrt(spread + EPS_NORM)
    return normed * (1.0 + scale_term[:, None, :]) + shift_term[:, None, :]

def round_trip(values):
    return lax.optimization_barrier(values.astype(jnp.bfloat16)).astype(jnp.float32)

def conv_bands(kernel):
    pixels = GRIDW * PATCH
    in_pixel = jnp.arange(pixels)[:, None]
    out_pixel = jnp.arange(pixels)[None, :]
    band_list = []
    for row_off in range(3):
        summed = jnp.zeros((pixels, CHANNELS, pixels, CHANNELS), jnp.float32)
        for col_off in range(3):
            shifted = (in_pixel == out_pixel + col_off - 1).astype(jnp.float32)
            summed = summed + shifted[:, None, :, None] * kernel[row_off, col_off][None, :, None, :]
        band_list.append(summed.reshape(pixels * CHANNELS, pixels * CHANNELS))
    return band_list

def reference(hidden, noisy_latent, tile_latent, timesteps, step_embedding, alpha_now, alpha_next, modulation, attention_in, attention_out, expand_weight, reduce_weight, noise_head, preview_kernel):
    tiles_all = tile_latent.shape[0]
    tile_steps = timesteps[tile_latent]
    conditioning = jax.nn.silu(step_embedding[tile_steps].astype(jnp.float32)).astype(jnp.bfloat16)
    adaptive = jnp.dot(conditioning, modulation.reshape(D, 8 * D), preferred_element_type=jnp.float32).reshape(tiles_all, 8, D)
    group_tiles = 32
    group_count = tiles_all // group_tiles
    tokens_grouped = hidden.reshape(group_count, group_tiles, TILE, D)
    adaptive_grouped = adaptive.reshape(group_count, group_tiles, 8, D)

    def attention_inputs(packed):
        tokens, rows_adapt = packed
        normed = modulate_tiles(tokens.astype(jnp.float32), rows_adapt[:, 0], rows_adapt[:, 1]).astype(jnp.bfloat16)
        triple = jnp.dot(normed.reshape(-1, D), attention_in.reshape(D, 3 * D), preferred_element_type=jnp.float32)
        return triple.astype(jnp.bfloat16).reshape(group_tiles, TILE, 3, D)
    triple = lax.map(attention_inputs, (tokens_grouped, adaptive_grouped)).reshape(tiles_all, TILE, 3, D)
    reach_tiles = MAXT - 1
    window = 2 * reach_tiles + 1
    pad_ids = jnp.full((reach_tiles,), -1, jnp.int32)
    padded_ids = jnp.concatenate([pad_ids, tile_latent.astype(jnp.int32), pad_ids])
    key_pairs = jnp.pad(triple[:, :, 1:], ((reach_tiles, reach_tiles), (0, 0), (0, 0), (0, 0)))
    scale_factor = HEAD_DIM ** (-0.5)

    def attend_tile(tile_index):
        queries = triple[tile_index, :, 0].reshape(TILE, HEADS, HEAD_DIM).astype(jnp.float32)
        nearby = lax.dynamic_slice_in_dim(key_pairs, tile_index, window, 0)
        nearby = nearby.reshape(window * TILE, 2, HEADS, HEAD_DIM).astype(jnp.float32)
        window_ids = lax.dynamic_slice_in_dim(padded_ids, tile_index, window, 0)
        allowed = jnp.repeat(window_ids == tile_latent[tile_index], TILE)
        scores = jnp.einsum('qhd,khd->hqk', queries, nearby[:, 0]) * scale_factor
        scores = jnp.where(allowed[None, None, :], scores, -1e+30)
        row_peak = lax.optimization_barrier(jnp.max(scores, axis=2, keepdims=True))
        raised = jnp.exp(scores - row_peak)
        weights = round_trip(raised / lax.optimization_barrier(jnp.sum(raised, axis=2, keepdims=True)))
        mixed = jnp.einsum('hqk,khd->qhd', weights, nearby[:, 1])
        return mixed.reshape(TILE, D).astype(jnp.bfloat16)
    attended = lax.map(attend_tile, jnp.arange(tiles_all, dtype=jnp.int32))
    attended_grouped = attended.reshape(group_count, group_tiles, TILE, D)
    cols_block = D // N_COL
    units_block = FF // N_COL

    def block_rest(packed):
        tokens, attended_rows, rows_adapt = packed
        flat_rows = attended_rows.reshape(-1, D)
        attn_sum = jnp.zeros((group_tiles * TILE, D), jnp.float32)
        for block_index in range(N_COL):
            part_rows = flat_rows[:, block_index * cols_block:(block_index + 1) * cols_block]
            part_weight = attention_out[block_index * cols_block:(block_index + 1) * cols_block]
            attn_sum = attn_sum + round_trip(jnp.dot(part_rows, part_weight, preferred_element_type=jnp.float32))
        residual = (tokens.astype(jnp.float32) + rows_adapt[:, 2][:, None, :] * attn_sum.reshape(group_tiles, TILE, D)).astype(jnp.bfloat16)
        normed_mid = modulate_tiles(residual.astype(jnp.float32), rows_adapt[:, 3], rows_adapt[:, 4]).astype(jnp.bfloat16)
        expanded = jnp.dot(normed_mid.reshape(-1, D), expand_weight, preferred_element_type=jnp.float32)
        activated = jax.nn.gelu(expanded, approximate=True).astype(jnp.bfloat16)
        mlp_sum = jnp.zeros((group_tiles * TILE, D), jnp.float32)
        for block_index in range(N_COL):
            part_rows = activated[:, block_index * units_block:(block_index + 1) * units_block]
            part_weight = reduce_weight[block_index * units_block:(block_index + 1) * units_block]
            mlp_sum = mlp_sum + round_trip(jnp.dot(part_rows, part_weight, preferred_element_type=jnp.float32))
        second = (residual.astype(jnp.float32) + rows_adapt[:, 5][:, None, :] * mlp_sum.reshape(group_tiles, TILE, D)).astype(jnp.bfloat16)
        normed_out = modulate_tiles(second.astype(jnp.float32), rows_adapt[:, 6], rows_adapt[:, 7]).astype(jnp.bfloat16)
        return jnp.dot(normed_out.reshape(-1, D), noise_head, preferred_element_type=jnp.float32)
    noise_pred = lax.map(block_rest, (tokens_grouped, attended_grouped, adaptive_grouped))
    noise_img = noise_pred.reshape(tiles_all, TILE_ROWS, GRIDW, PATCH, PATCH, CHANNELS)
    noise_img = noise_img.transpose(0, 1, 3, 2, 4, 5).reshape(LROWS, LWIDTH)
    row_latent = jnp.repeat(tile_latent.astype(jnp.int32), TILE_ROWS * PATCH)
    row_steps = timesteps[row_latent]
    signal_now = alpha_now[row_steps][:, None]
    signal_next = alpha_next[row_steps][:, None]
    noisy_rows = noisy_latent.astype(jnp.float32)
    clean_rows = (noisy_rows - jnp.sqrt(1.0 - signal_now) * noise_img) / jnp.sqrt(signal_now)
    stepped = (jnp.sqrt(signal_next) * clean_rows + jnp.sqrt(1.0 - signal_next) * noise_img).astype(jnp.bfloat16)
    band_list = conv_bands(preview_kernel)
    empty_row = jnp.zeros((1, LWIDTH), jnp.float32)
    above_rows = jnp.concatenate([empty_row, clean_rows[:-1]], axis=0)
    below_rows = jnp.concatenate([clean_rows[1:], empty_row], axis=0)
    edge_id = jnp.full((1,), -1, jnp.int32)
    above_ok = (jnp.concatenate([edge_id, row_latent[:-1]]) == row_latent)[:, None]
    below_ok = (jnp.concatenate([row_latent[1:], edge_id]) == row_latent)[:, None]
    highest = lax.Precision.HIGHEST
    preview = jnp.where(above_ok, jnp.dot(above_rows, band_list[0], precision=highest), 0.0) + jnp.dot(clean_rows, band_list[1], precision=highest) + jnp.where(below_ok, jnp.dot(below_rows, band_list[2], precision=highest), 0.0)
    return (stepped, preview.astype(jnp.bfloat16))
```

```python
import jax
import jax.numpy as jnp
from jax import lax
from jax.sharding import PartitionSpec as P

D = 1152
HEAD_DIM = 72
PATCH = 2
CHANNELS = 4
GRIDW = 16
TILE_ROWS = 8
STEPS = 50
TILE = 128
EPS_NORM = 1e-06


def exchange(value, axis, offset):
    size = lax.axis_size(axis)
    return lax.ppermute(value, axis, [(i, i ^ offset) for i in range(size)])


def gather_blocks(value):
    across = exchange(value, "col", 2)
    beside = exchange(value, "col", 1)
    diagonal = exchange(across, "col", 1)
    return value, beside, across, diagonal


def natural_order(blocks, axis):
    own, beside, across, diagonal = blocks
    col_index = lax.axis_index("col")
    odd = col_index % 2 == 1
    upper = col_index // 2 == 1
    near = jnp.where(odd, jnp.concatenate([beside, own], axis), jnp.concatenate([own, beside], axis))
    far = jnp.where(
        odd, jnp.concatenate([diagonal, across], axis), jnp.concatenate([across, diagonal], axis)
    )
    return jnp.where(upper, jnp.concatenate([far, near], axis), jnp.concatenate([near, far], axis))


def gather_rows(block):
    rows = lax.axis_size("row")
    if rows != 8:
        return lax.all_gather(block, "row", axis=0)
    pieces = {0: block}
    pieces[4] = exchange(block, "row", 4)
    pieces[2] = exchange(block, "row", 2)
    pieces[1] = exchange(block, "row", 1)
    pieces[3] = exchange(pieces[2], "row", 1)
    pieces[6] = exchange(pieces[4], "row", 2)
    pieces[5] = exchange(pieces[4], "row", 1)
    pieces[7] = exchange(pieces[6], "row", 1)
    here = lax.axis_index("row")
    whole = jnp.zeros((rows,) + block.shape, block.dtype)
    for offset in range(rows):
        whole = lax.dynamic_update_index_in_dim(whole, pieces[offset], here ^ offset, 0)
    return whole


def normalize(values, shift_term, scale_term):
    mean_value = jnp.sum(values, axis=-1, keepdims=True) / D
    spread = jnp.sum(values * values, axis=-1, keepdims=True) / D - mean_value * mean_value
    normed = (values - mean_value) * lax.rsqrt(spread + EPS_NORM)
    return normed * (1.0 + scale_term) + shift_term


def conv_bands(kernel):
    pixels = GRIDW * PATCH
    in_pixel = jnp.arange(pixels)[:, None]
    out_pixel = jnp.arange(pixels)[None, :]
    band_list = []
    for row_off in range(3):
        summed = jnp.zeros((pixels, CHANNELS, pixels, CHANNELS), jnp.float32)
        for col_off in range(3):
            shifted = (in_pixel == out_pixel + col_off - 1).astype(jnp.float32)
            summed = summed + shifted[:, None, :, None] * kernel[row_off, col_off][None, :, None, :]
        band_list.append(summed.reshape(pixels * CHANNELS, pixels * CHANNELS))
    return band_list


def shards(
    hidden,
    noisy_latent,
    tile_latent,
    timesteps,
    step_embedding,
    alpha_now,
    alpha_next,
    modulation,
    attention_in,
    attention_out,
    expand_weight,
    reduce_weight,
    noise_head,
    preview_kernel,
):
    wide = jnp.float32
    narrow = jnp.bfloat16
    rows = lax.axis_size("row")
    token_count, cols_here = hidden.shape
    tiles_here = token_count // TILE
    heads_here = cols_here // HEAD_DIM
    row_index = lax.axis_index("row")
    col_index = lax.axis_index("col")

    hidden_blocks = gather_blocks(hidden)

    ends = tile_latent.reshape(rows, tiles_here)[:, jnp.array([0, tiles_here - 1])].reshape(-1)
    latent_range = jnp.arange(timesteps.shape[0], dtype=jnp.int32)
    end_steps = jnp.sum(jnp.where(ends[:, None] == latent_range[None, :], timesteps[None, :], 0), axis=1)
    step_range = jnp.arange(STEPS, dtype=jnp.int32)
    depth = modulation.shape[0]
    embedding_here = lax.dynamic_slice_in_dim(step_embedding, row_index * depth, depth, 1)
    embedded = jnp.dot(
        (end_steps[:, None] == step_range[None, :]).astype(narrow),
        embedding_here,
        preferred_element_type=wide,
    )
    conditioning = jax.nn.silu(embedded).astype(narrow)
    partial = jnp.einsum("td,dkc->tkc", conditioning, modulation, preferred_element_type=wide)
    partial = partial.reshape(rows, 2, 8 * cols_here)
    adaptive = jnp.sum(lax.all_to_all(partial, "row", 0, 0, tiled=True), axis=0)
    adaptive = lax.all_gather(adaptive, "col", axis=0).reshape(-1, 2, 8, cols_here)
    adaptive = adaptive.transpose(1, 2, 0, 3).reshape(2, 8, D)

    weights_here = jnp.concatenate([expand_weight, reduce_weight.T], axis=0)
    out_weight = lax.all_gather(attention_out, "col", axis=0, tiled=True)
    gathered = gather_rows(weights_here)
    expand_all = gathered[:, :depth].reshape(D, -1)
    reduce_all = gathered[:, depth:].reshape(D, -1)

    my_latent = lax.dynamic_slice_in_dim(tile_latent, row_index * tiles_here, tiles_here)
    second_latent = my_latent != my_latent[0]
    per_tile = jnp.where(second_latent[:, None, None], adaptive[1][None], adaptive[0][None])
    term = lambda index: per_tile[:, index][:, None, :]

    tokens = natural_order(hidden_blocks, 1).astype(wide).reshape(tiles_here, TILE, D)
    normed_in = normalize(tokens, term(0), term(1)).astype(narrow).reshape(token_count, D)
    triple = jnp.einsum("td,dsc->tsc", normed_in, attention_in, preferred_element_type=wide)
    triple = triple.astype(narrow)
    queries = triple[:, 0]
    key_pairs = triple[:, 1:]
    allowed = my_latent[:, None] == my_latent[None, :]
    token_allowed = jnp.repeat(jnp.repeat(allowed, TILE, axis=0), TILE, axis=1)
    scale_factor = HEAD_DIM ** (-0.5)
    head_outputs = []
    for head_index in range(heads_here):
        lower = head_index * HEAD_DIM
        query_head = queries[:, lower : lower + HEAD_DIM]
        key_head = key_pairs[:, 0, lower : lower + HEAD_DIM]
        value_head = key_pairs[:, 1, lower : lower + HEAD_DIM]
        scores = (
            jnp.einsum("qd,kd->qk", query_head, key_head, preferred_element_type=wide)
            * scale_factor
        )
        scores = jnp.where(token_allowed, scores, -1e30)
        row_peak = jnp.max(scores, axis=1, keepdims=True)
        raised = jnp.exp(scores - row_peak)
        weights = (raised / jnp.sum(raised, axis=1, keepdims=True)).astype(narrow)
        mixed = jnp.dot(weights, value_head, preferred_element_type=wide)
        head_outputs.append(mixed.astype(narrow))
    attended_here = jnp.concatenate(head_outputs, axis=1)
    attended = natural_order(gather_blocks(attended_here), 1)
    attn_sum = jnp.dot(attended, out_weight, preferred_element_type=wide)
    residual = tokens + term(2) * attn_sum.reshape(tiles_here, TILE, D)
    residual = residual.astype(narrow)
    normed_mid = normalize(residual.astype(wide), term(3), term(4)).astype(narrow)

    def mlp_tiles(tile_list):
        rows_in = jnp.concatenate(
            [lax.dynamic_index_in_dim(normed_mid, index, 0, keepdims=False) for index in tile_list]
        )
        expanded = jnp.dot(rows_in, expand_all, preferred_element_type=wide)
        activated = jax.nn.gelu(expanded, approximate=True).astype(narrow)
        summed = lax.dot_general(
            activated, reduce_all, (((1,), (1,)), ((), ())), preferred_element_type=wide
        )
        return summed.reshape(len(tile_list), TILE, D)

    far = mlp_tiles([col_index ^ 2, col_index ^ 3])
    far_sum = far[0] + exchange(far[1].astype(narrow), "col", 1).astype(wide)
    crossed = exchange(far_sum.astype(narrow), "col", 2)
    near = mlp_tiles([col_index, col_index ^ 1])
    near_sum = near[0] + exchange(near[1].astype(narrow), "col", 1).astype(wide)
    mlp_sum = near_sum + crossed.astype(wide)
    own_tile = lambda array: lax.dynamic_index_in_dim(array, col_index, 0, keepdims=False)
    own_terms = own_tile(per_tile)
    second = own_tile(residual).astype(wide) + own_terms[5][None] * mlp_sum
    second = second.astype(narrow).astype(wide)
    normed_out = normalize(second, own_terms[6][None], own_terms[7][None]).astype(narrow)
    noise_weight = lax.all_gather(noise_head, "col", axis=0, tiled=True)
    noise_tile = jnp.dot(normed_out, noise_weight, preferred_element_type=wide)
    noise_tile = noise_tile.reshape(TILE_ROWS, GRIDW, PATCH, PATCH * CHANNELS)
    noise_tile = noise_tile.transpose(0, 2, 1, 3).reshape(TILE_ROWS * PATCH, -1)
    noise_img = lax.all_gather(noise_tile, "col", axis=0, tiled=True)

    rows_per_tile = TILE_ROWS * PATCH
    my_steps = jnp.sum(jnp.where(my_latent[:, None] == latent_range[None, :], timesteps[None, :], 0), axis=1)
    step_match = my_steps[:, None] == step_range[None, :]
    tile_now = jnp.sum(jnp.where(step_match, alpha_now[None, :], 0.0), axis=1)
    tile_next = jnp.sum(jnp.where(step_match, alpha_next[None, :], 0.0), axis=1)
    signal_now = jnp.repeat(tile_now, rows_per_tile)[:, None]
    signal_next = jnp.repeat(tile_next, rows_per_tile)[:, None]
    noisy_rows = noisy_latent.astype(wide)
    clean_rows = (noisy_rows - jnp.sqrt(1.0 - signal_now) * noise_img) / jnp.sqrt(signal_now)
    stepped = (jnp.sqrt(signal_next) * clean_rows + jnp.sqrt(1.0 - signal_next) * noise_img).astype(
        narrow
    )
    framed = jnp.pad(clean_rows, ((1, 1), (0, 0)))
    edge_pad = jnp.full((1,), -1, jnp.int32)
    row_latent = jnp.repeat(my_latent, rows_per_tile)
    above_ok = (jnp.concatenate([edge_pad, row_latent[:-1]]) == row_latent)[:, None]
    below_ok = (jnp.concatenate([row_latent[1:], edge_pad]) == row_latent)[:, None]
    band_list = conv_bands(preview_kernel)
    highest = lax.Precision.HIGHEST
    preview = (
        jnp.where(above_ok, jnp.dot(framed[:-2], band_list[0], precision=highest), 0.0)
        + jnp.dot(clean_rows, band_list[1], precision=highest)
        + jnp.where(below_ok, jnp.dot(framed[2:], band_list[2], precision=highest), 0.0)
    )
    return (stepped, preview.astype(narrow))


def solution(mesh):
    return jax.shard_map(
        shards,
        mesh=mesh,
        in_specs=(
            P("row", "col"),
            P("row", None),
            P(),
            P(),
            P(),
            P(),
            P(),
            P("row", None, "col"),
            P(None, None, "col"),
            P("col", None),
            P("row", "col"),
            P("col", "row"),
            P("col", None),
            P(),
        ),
        out_specs=(P("row", None), P("row", None)),
        check_vma=False,
    )
```

```python
import functools

import jax
import jax.numpy as jnp
from jax import lax
from jax.experimental import pallas as pl
from jax.experimental.pallas import tpu as pltpu
from jax.sharding import PartitionSpec as P

D = 1152
HEAD_DIM = 72
PATCH = 2
CHANNELS = 4
GRIDW = 16
TILE_ROWS = 8
STEPS = 50
TILE = 128
EPS_NORM = 1e-06
IMG_ROWS = TILE_ROWS * PATCH
IMG_WIDTH = GRIDW * PATCH * CHANNELS
WIDE = jnp.float32
NARROW = jnp.bfloat16
NT = (((1,), (1,)), ((), ()))
VMEM = pl.BlockSpec(memory_space=pltpu.VMEM)
SMEM = pl.BlockSpec(memory_space=pltpu.SMEM)
ANYWHERE = pl.BlockSpec(memory_space=pl.ANY)
VMEM_LIMIT = 40 * 1024 * 1024


def call(kernel, outs, in_specs, scratch=(), flops=0, nbytes=0, trans=0):
    return pl.pallas_call(
        kernel,
        out_shape=outs,
        in_specs=in_specs,
        out_specs=jax.tree.map(lambda _: VMEM, outs),
        scratch_shapes=list(scratch),
        compiler_params=pltpu.CompilerParams(vmem_limit_bytes=VMEM_LIMIT),
        cost_estimate=pl.CostEstimate(flops=flops, bytes_accessed=nbytes, transcendentals=trans),
    )


def exchange(value, axis, offset):
    size = lax.axis_size(axis)
    return lax.ppermute(value, axis, [(i, i ^ offset) for i in range(size)])


def gather_blocks(value):
    across = exchange(value, "col", 2)
    beside = exchange(value, "col", 1)
    diagonal = exchange(across, "col", 1)
    return value, beside, across, diagonal


def gather_rows(block):
    rows = lax.axis_size("row")
    if rows != 8:
        half = block.shape[0] // 2
        whole = lax.all_gather(block, "row", axis=0)
        return [jnp.concatenate([whole[:, :half], whole[:, half:]]).reshape(-1, block.shape[1])]
    pieces = {0: block}
    pieces[4] = exchange(block, "row", 4)
    pieces[2] = exchange(block, "row", 2)
    pieces[1] = exchange(block, "row", 1)
    pieces[3] = exchange(pieces[2], "row", 1)
    pieces[6] = exchange(pieces[4], "row", 2)
    pieces[5] = exchange(pieces[4], "row", 1)
    pieces[7] = exchange(pieces[6], "row", 1)
    return [pieces[offset] for offset in range(rows)]


def normalize(values, shift_term, scale_term):
    mean_value = jnp.sum(values, axis=-1, keepdims=True) * (1.0 / D)
    spread = jnp.sum(values * values, axis=-1, keepdims=True) * (1.0 / D) - mean_value * mean_value
    normed = (values - mean_value) * lax.rsqrt(spread + EPS_NORM)
    return normed * (1.0 + scale_term) + shift_term


def condition_kernel(tiles_here, latent_ref, steps_ref, embedding_ref, out_ref, onehot):
    count, depth = out_ref.shape

    def pick(index, carry):
        tile = (index // 2) * tiles_here + (index % 2) * (tiles_here - 1)
        step = steps_ref[latent_ref[tile]]
        lanes = lax.broadcasted_iota(jnp.int32, (1, STEPS), 1)
        onehot[pl.ds(index, 1), :] = jnp.where(lanes == step, 1.0, 0.0)
        return carry

    lax.fori_loop(0, count, pick, 0)
    embedded = jnp.dot(onehot[...].astype(NARROW), embedding_ref[...], preferred_element_type=WIDE)
    conditioning = (embedded / (1.0 + jnp.exp(-embedded))).astype(NARROW)
    first = lax.axis_index("row") * depth
    source = lax.broadcasted_iota(jnp.int32, (D, depth), 0)
    target = lax.broadcasted_iota(jnp.int32, (D, depth), 1) + first
    chosen = jnp.where(source == target, 1.0, 0.0).astype(NARROW)
    out_ref[...] = jnp.dot(conditioning, chosen, preferred_element_type=WIDE).astype(NARROW)


def tile_term(latent_ref, terms_ref, index, tile):
    first = lax.axis_index("row") * (lax.axis_size("col"))
    later = latent_ref[first + tile] != latent_ref[first]
    return jnp.where(later, terms_ref[8 + index : 9 + index, :], terms_ref[index : index + 1, :])


def attention_kernel(
    latent_ref, own, beside, across, diagonal, gathered_ref, weight_ref,
    tokens_ref, terms_ref, attended_ref, normed, triple,
):
    col = lax.axis_index("col")
    row = lax.axis_index("row")
    width = own.shape[1]
    tiles = own.shape[0] // TILE
    for place in range(4):
        terms_ref[:, place * width : (place + 1) * width] = gathered_ref[place]

        @pl.when(col == place)
        def _():
            for offset, block in enumerate((own, beside, across, diagonal)):
                lower = (place ^ offset) * width
                tokens_ref[:, lower : lower + width] = block[...]

    for tile in range(tiles):
        here = slice(tile * TILE, (tile + 1) * TILE)
        shift = tile_term(latent_ref, terms_ref, 0, tile)
        scale = tile_term(latent_ref, terms_ref, 1, tile)
        normed[here, :] = normalize(tokens_ref[here, :].astype(WIDE), shift, scale).astype(NARROW)
    triple[...] = jnp.dot(normed[...], weight_ref[...], preferred_element_type=WIDE).astype(NARROW)
    key_tile = lax.broadcasted_iota(jnp.int32, (1, tiles * TILE), 1) // TILE
    key_latent = jnp.zeros((1, tiles * TILE), jnp.int32)
    for tile in range(tiles):
        key_latent = jnp.where(key_tile == tile, latent_ref[row * tiles + tile], key_latent)
    factor = HEAD_DIM ** (-0.5) * 1.4426950408889634
    for head in range(width // HEAD_DIM):
        lower = head * HEAD_DIM
        keys = triple[:, width + lower : width + lower + HEAD_DIM]
        mixed_values = triple[:, 2 * width + lower : 2 * width + lower + HEAD_DIM]
        for tile in range(tiles):
            here = slice(tile * TILE, (tile + 1) * TILE)
            barred = jnp.where(key_latent == latent_ref[row * tiles + tile], 0.0, -1e30)
            scores = lax.dot_general(
                triple[here, lower : lower + HEAD_DIM], keys, NT, preferred_element_type=WIDE
            )
            scores = scores + barred
            peak = jnp.max(scores, axis=1, keepdims=True)
            raised = jnp.exp2((scores - peak) * factor)
            total = jnp.sum(raised, axis=1, keepdims=True)
            mixed = jnp.dot(raised.astype(NARROW), mixed_values, preferred_element_type=WIDE)
            attended_ref[here, lower : lower + HEAD_DIM] = (mixed / total).astype(NARROW)


def mlp_kernel(near, depth, latent_ref, att_own, att_beside, att_across, att_diagonal, tokens_ref, terms_ref, *refs):
    out_blocks, refs = refs[:4], refs[4:]
    count = len(refs) - (3 if near else 2) - 7
    pieces, refs = refs[:count], refs[count:]
    outs, scratch = refs[:-7], refs[-7:]
    out_weight, expand, reduce, attended, mid, out_sems, piece_sems = scratch
    col = lax.axis_index("col")
    row = lax.axis_index("row")
    width = att_own.shape[1]
    out_copies = []
    for offset, block in enumerate(out_blocks):
        start = pl.multiple_of((col ^ offset) * width, 16)
        out_copies.append(
            pltpu.make_async_copy(block, out_weight.at[pl.ds(start, width), :], out_sems.at[offset])
        )
    piece_copies = []
    for offset, piece in enumerate(pieces):
        start = pl.multiple_of((row ^ offset) * depth, 16) if count > 1 else 0
        for half, target in enumerate((expand, reduce)):
            piece_copies.append(
                pltpu.make_async_copy(
                    piece.at[pl.ds(half * depth, depth), :],
                    target.at[pl.ds(start, depth), :],
                    piece_sems.at[2 * offset + half],
                )
            )
    for copy in out_copies + piece_copies:
        copy.start()
    tile_offsets = (0, 1) if near else (2, 3)
    for place in range(4):

        @pl.when(col == place)
        def _():
            for offset, block in enumerate((att_own, att_beside, att_across, att_diagonal)):
                lower = (place ^ offset) * width
                for slot, tile_offset in enumerate(tile_offsets):
                    first = (place ^ tile_offset) * TILE
                    attended[slot * TILE : (slot + 1) * TILE, lower : lower + width] = block[
                        first : first + TILE, :
                    ]

    for copy in out_copies:
        copy.wait()
    attn_sum = jnp.dot(attended[...], out_weight[...], preferred_element_type=WIDE)
    for slot, tile_offset in enumerate(tile_offsets):
        tile = col ^ tile_offset
        term = functools.partial(tile_term, latent_ref, terms_ref, tile=tile)
        here = slice(slot * TILE, (slot + 1) * TILE)
        before = tokens_ref[pl.ds(pl.multiple_of(tile * TILE, TILE), TILE), :].astype(WIDE)
        residual = (before + term(2) * attn_sum[here]).astype(NARROW)
        if near and slot == 0:
            outs[2][...] = residual
        mid[here, :] = normalize(residual.astype(WIDE), term(3), term(4)).astype(NARROW)
    for copy in piece_copies:
        copy.wait()
    units = jnp.dot(mid[...], expand[...], preferred_element_type=WIDE)
    inner = 0.7978845608028654 * (units + 0.044715 * (units * units * units))
    activated = (0.5 * units * (1.0 + jnp.tanh(inner))).astype(NARROW)
    summed = lax.dot_general(activated, reduce[...], NT, preferred_element_type=WIDE)
    outs[0][...] = summed[:TILE]
    outs[1][...] = summed[TILE:].astype(NARROW)


def head_kernel(latent_ref, kept_ref, beside_ref, crossed_ref, residual_ref, terms_ref, out_ref):
    col = lax.axis_index("col")
    term = functools.partial(tile_term, latent_ref, terms_ref, tile=col)
    mlp_sum = kept_ref[...] + beside_ref[...].astype(WIDE) + crossed_ref[...].astype(WIDE)
    second = (residual_ref[...].astype(WIDE) + term(5) * mlp_sum).astype(NARROW).astype(WIDE)
    normed = normalize(second, term(6), term(7)).astype(NARROW)
    group = PATCH * CHANNELS
    token_place = lax.broadcasted_iota(jnp.int32, (TILE, IMG_WIDTH), 0) % GRIDW
    lane_place = lax.broadcasted_iota(jnp.int32, (TILE, IMG_WIDTH), 1) // group
    for dy in range(PATCH):
        rows = terms_ref[16 + dy * group : 16 + (dy + 1) * group, :].astype(NARROW)
        spread_rows = jnp.concatenate([rows.astype(WIDE)] * GRIDW, axis=0).astype(NARROW)
        noise = lax.dot_general(normed, spread_rows, NT, preferred_element_type=WIDE)
        noise = jnp.where(token_place == lane_place, noise, 0.0)
        folded = jnp.sum(noise.reshape(TILE_ROWS, GRIDW, IMG_WIDTH), axis=1)
        out_ref[:, dy * IMG_WIDTH : (dy + 1) * IMG_WIDTH] = folded


def bands_kernel(kernel_ref, out_ref):
    shape = (IMG_WIDTH, IMG_WIDTH)
    source = lax.broadcasted_iota(jnp.int32, shape, 0)
    target = lax.broadcasted_iota(jnp.int32, shape, 1)
    reach = 3 * CHANNELS
    apart = target - (source // CHANNELS) * CHANNELS + CHANNELS
    code = jnp.where((apart >= 0) & (apart < reach), (source % CHANNELS) * reach + apart, -1)
    bands = [jnp.zeros(shape, WIDE) for _ in range(3)]
    for channel in range(CHANNELS):
        for lane in range(reach):
            here = code == channel * reach + lane
            column, out_channel = 2 - lane // CHANNELS, lane % CHANNELS
            for line in range(3):
                place = ((line * 3 + column) * CHANNELS + channel) * CHANNELS + out_channel
                bands[line] = jnp.where(here, kernel_ref[place], bands[line])
    for line in range(3):
        out_ref[:, line * IMG_WIDTH : (line + 1) * IMG_WIDTH] = bands[line]


def step_kernel(
    latent_ref, steps_ref, now_ref, next_ref, noise_ref, noisy_ref, bands_ref,
    stepped_ref, preview_ref, image, clean, above, below,
):
    tiles = noise_ref.shape[0]
    row = lax.axis_index("row")
    for tile in range(tiles):
        for dy in range(PATCH):
            image[pl.ds(tile * IMG_ROWS + dy, TILE_ROWS, PATCH), :] = noise_ref[
                tile, :, dy * IMG_WIDTH : (dy + 1) * IMG_WIDTH
            ]
    for tile in range(tiles):
        here = slice(tile * IMG_ROWS, (tile + 1) * IMG_ROWS)
        step = steps_ref[latent_ref[row * tiles + tile]]
        signal_now = jnp.full((1, IMG_WIDTH), now_ref[step], WIDE)
        signal_next = jnp.full((1, IMG_WIDTH), next_ref[step], WIDE)
        noise = image[here, :]
        rows = (noisy_ref[here, :].astype(WIDE) - jnp.sqrt(1.0 - signal_now) * noise) / jnp.sqrt(signal_now)
        clean[here, :] = rows
        stepped = jnp.sqrt(signal_next) * rows + jnp.sqrt(1.0 - signal_next) * noise
        stepped_ref[here, :] = stepped.astype(NARROW)
    parts = jnp.dot(
        clean[...], bands_ref[...], precision=lax.Precision.HIGHEST, preferred_element_type=WIDE
    )
    count = tiles * IMG_ROWS
    above[8 : 8 + count, :] = parts[:, :IMG_WIDTH]
    below[8 : 8 + count, :] = parts[:, 2 * IMG_WIDTH :]
    for tile in range(tiles):
        here = slice(tile * IMG_ROWS, (tile + 1) * IMG_ROWS)
        start = 8 + tile * IMG_ROWS
        line = lax.broadcasted_iota(jnp.int32, (IMG_ROWS, IMG_WIDTH), 0)
        from_above = above[start - 1 : start - 1 + IMG_ROWS, :]
        from_below = below[start + 1 : start + 1 + IMG_ROWS, :]
        mine = latent_ref[row * tiles + tile]
        if tile == 0:
            above_ok = line > 0
        else:
            above_ok = (line > 0) | (latent_ref[row * tiles + tile - 1] == mine)
        if tile == tiles - 1:
            below_ok = line < IMG_ROWS - 1
        else:
            below_ok = (line < IMG_ROWS - 1) | (latent_ref[row * tiles + tile + 1] == mine)
        total = parts[here, IMG_WIDTH : 2 * IMG_WIDTH]
        total = total + jnp.where(above_ok, from_above, 0.0) + jnp.where(below_ok, from_below, 0.0)
        preview_ref[here, :] = total.astype(NARROW)


def shards(
    hidden,
    noisy_latent,
    tile_latent,
    timesteps,
    step_embedding,
    alpha_now,
    alpha_next,
    modulation,
    attention_in,
    attention_out,
    expand_weight,
    reduce_weight,
    noise_head,
    preview_kernel,
):
    rows = lax.axis_size("row")
    tokens_here, width = hidden.shape
    tiles = tokens_here // TILE
    depth = modulation.shape[0]
    units = expand_weight.shape[1]
    shape = jax.ShapeDtypeStruct

    hidden_blocks = gather_blocks(hidden)
    weights_here = jnp.concatenate([expand_weight, reduce_weight.T], axis=0)

    conditioning = call(
        functools.partial(condition_kernel, tiles),
        shape((2 * rows, depth), NARROW),
        [SMEM, SMEM, VMEM],
        [pltpu.VMEM((2 * rows, STEPS), WIDE)],
        flops=2 * 2 * rows * D * (STEPS + depth), nbytes=2 * STEPS * D,
    )(tile_latent, timesteps, step_embedding)
    partial = jnp.einsum("td,dkc->tkc", conditioning, modulation, preferred_element_type=WIDE)
    partial = partial.reshape(rows, 2, 8, width)
    adaptive = jnp.sum(lax.all_to_all(partial, "row", 0, 0, tiled=True), axis=0)
    shared = jnp.concatenate([adaptive.reshape(16, width), noise_head.T.astype(WIDE)])
    shared = lax.all_gather(shared, "col", axis=0)

    out_source, _ = lax.optimization_barrier((attention_out, hidden_blocks[2]))
    out_blocks = gather_blocks(out_source)
    pieces = gather_rows(weights_here)

    bands = call(
        bands_kernel, shape((IMG_WIDTH, 3 * IMG_WIDTH), WIDE), [SMEM], flops=10**8, nbytes=3 * 2**16
    )(preview_kernel.reshape(-1))

    tokens, terms, attended = call(
        attention_kernel,
        [shape((tokens_here, D), NARROW), shape((32, D), WIDE), shape((tokens_here, width), NARROW)],
        [SMEM] + [VMEM] * 6,
        [pltpu.VMEM((tokens_here, D), NARROW), pltpu.VMEM((tokens_here, 3 * width), NARROW)],
        flops=2 * tokens_here * (D * 3 * width + 2 * tokens_here * width), nbytes=5 * 2**20,
        trans=4 * tokens_here**2,
    )(tile_latent, *hidden_blocks, shared, attention_in.reshape(D, 3 * width))
    attended_blocks = gather_blocks(attended)

    def mlp(near):
        outs = [shape((TILE, D), WIDE), shape((TILE, D), NARROW)]
        if near:
            outs.append(shape((TILE, D), NARROW))
        piece_depth = pieces[0].shape[0] // 2
        return call(
            functools.partial(mlp_kernel, near, piece_depth),
            outs,
            [SMEM] + [VMEM] * 6 + [ANYWHERE] * (4 + len(pieces)),
            [
                pltpu.VMEM((D, D), NARROW),
                pltpu.VMEM((D, units), NARROW),
                pltpu.VMEM((D, units), NARROW),
                pltpu.VMEM((2 * TILE, D), NARROW),
                pltpu.VMEM((2 * TILE, D), NARROW),
                pltpu.SemaphoreType.DMA((4,)),
                pltpu.SemaphoreType.DMA((2 * len(pieces),)),
            ],
            flops=4 * TILE * D * (D + 2 * units), nbytes=8 * 2**20, trans=2 * TILE * units,
        )(tile_latent, *attended_blocks, tokens, terms, *out_blocks, *pieces)

    far_kept, far_sent = mlp(False)
    far_sum = (far_kept + exchange(far_sent, "col", 1).astype(WIDE)).astype(NARROW)
    crossed = exchange(far_sum, "col", 2)
    near_kept, near_sent, residual = mlp(True)
    beside = exchange(near_sent, "col", 1)
    noise = call(
        head_kernel,
        shape((TILE_ROWS, PATCH * IMG_WIDTH), WIDE),
        [SMEM] + [VMEM] * 5,
        flops=4 * TILE * D * IMG_WIDTH, nbytes=2**21,
    )(tile_latent, near_kept, beside, crossed, residual, terms)
    noise = lax.all_gather(noise, "col", axis=0)

    img_rows = tiles * IMG_ROWS
    stepped, preview = call(
        step_kernel,
        [shape((img_rows, IMG_WIDTH), NARROW)] * 2,
        [SMEM] * 4 + [VMEM] * 3,
        [pltpu.VMEM((img_rows, IMG_WIDTH), WIDE)] * 2
        + [pltpu.VMEM((img_rows + 16, IMG_WIDTH), WIDE)] * 2,
        flops=12 * img_rows * IMG_WIDTH**2, nbytes=2**19,
    )(tile_latent, timesteps, alpha_now, alpha_next, noise, noisy_latent, bands)
    return (stepped, preview)


def solution(mesh):
    return jax.shard_map(
        shards,
        mesh=mesh,
        in_specs=(
            P("row", "col"),
            P("row", None),
            P(),
            P(),
            P(),
            P(),
            P(),
            P("row", None, "col"),
            P(None, None, "col"),
            P("col", None),
            P("row", "col"),
            P("col", "row"),
            P("col", None),
            P(),
        ),
        out_specs=(P("row", None), P("row", None)),
        check_vma=False,
    )
```

```python
import functools

import jax
import jax.numpy as jnp
from jax import lax
from jax.experimental import pallas as pl
from jax.experimental.pallas import tpu as pltpu
from jax.sharding import PartitionSpec as P

D = 1152
HEAD_DIM = 72
PATCH = 2
CHANNELS = 4
GRIDW = 16
TILE_ROWS = 8
STEPS = 50
TILE = 128
EPS_NORM = 1e-06
IMG_ROWS = TILE_ROWS * PATCH
IMG_WIDTH = GRIDW * PATCH * CHANNELS
WIDE = jnp.float32
NARROW = jnp.bfloat16
NT = (((1,), (1,)), ((), ()))
VMEM = pl.BlockSpec(memory_space=pltpu.VMEM)
SMEM = pl.BlockSpec(memory_space=pltpu.SMEM)
ANYWHERE = pl.BlockSpec(memory_space=pl.ANY)
MIB = 1024 * 1024


def call(kernel, outs, in_specs, scratch=(), flops=0, nbytes=0, trans=0, limit=4):
    return pl.pallas_call(
        kernel,
        out_shape=outs,
        in_specs=in_specs,
        out_specs=jax.tree.map(lambda _: VMEM, outs),
        scratch_shapes=list(scratch),
        compiler_params=pltpu.CompilerParams(vmem_limit_bytes=limit * MIB),
        cost_estimate=pl.CostEstimate(flops=flops, bytes_accessed=nbytes, transcendentals=trans),
    )


def exchange(value, axis, offset):
    size = lax.axis_size(axis)
    return lax.ppermute(value, axis, [(i, i ^ offset) for i in range(size)])


def gather_blocks(value):
    across = exchange(value, "col", 2)
    beside = exchange(value, "col", 1)
    diagonal = exchange(across, "col", 1)
    return value, beside, across, diagonal


def gather_late(value, late):
    across = exchange(value, "col", 2)
    value, across = after((value, across), late)
    return value, exchange(value, "col", 1), across, exchange(across, "col", 1)


def after(value, *others):
    return lax.optimization_barrier((value, *others))[0]


def gather_rows(expand, reduce):
    if lax.axis_size("row") != 8:
        return [[lax.all_gather(part, "row", axis=0, tiled=True) for part in (expand, reduce)]]
    pieces = {0: jnp.concatenate([expand, reduce], axis=0)}
    for offset, source, step in ((4, 0, 4), (2, 0, 2), (1, 0, 1), (6, 4, 2), (3, 2, 1), (5, 4, 1), (7, 6, 1)):
        pieces[offset] = exchange(pieces[source], "row", step)
    return [[pieces[offset]] for offset in range(8)]


def normalize(values, shift_term, scale_term):
    mean_value = jnp.sum(values, axis=-1, keepdims=True) * (1.0 / D)
    spread = jnp.sum(values * values, axis=-1, keepdims=True) * (1.0 / D) - mean_value * mean_value
    normed = (values - mean_value) * lax.rsqrt(spread + EPS_NORM)
    return normed * (1.0 + scale_term) + shift_term


def condition_kernel(tiles_here, latent_ref, steps_ref, embedding_ref, out_ref, onehot):
    count, depth = out_ref.shape

    def pick(index, carry):
        tile = (index // 2) * tiles_here + (index % 2) * (tiles_here - 1)
        step = steps_ref[latent_ref[tile]]
        lanes = lax.broadcasted_iota(jnp.int32, (1, STEPS), 1)
        onehot[pl.ds(index, 1), :] = jnp.where(lanes == step, 1.0, 0.0)
        return carry

    lax.fori_loop(0, count, pick, 0)
    embedded = jnp.dot(onehot[...].astype(NARROW), embedding_ref[...], preferred_element_type=WIDE)
    conditioning = (embedded / (1.0 + jnp.exp(-embedded))).astype(NARROW)
    first = lax.axis_index("row") * depth
    source = lax.broadcasted_iota(jnp.int32, (D, depth), 0)
    target = lax.broadcasted_iota(jnp.int32, (D, depth), 1) + first
    chosen = jnp.where(source == target, 1.0, 0.0).astype(NARROW)
    out_ref[...] = jnp.dot(conditioning, chosen, preferred_element_type=WIDE).astype(NARROW)


def tile_term(latent_ref, terms_ref, index, tile):
    first = lax.axis_index("row") * (lax.axis_size("col"))
    later = latent_ref[first + tile] != latent_ref[first]
    return jnp.where(later, terms_ref[8 + index : 9 + index, :], terms_ref[index : index + 1, :])


def tokens_kernel(own, beside, across, diagonal, kernel_ref, tokens_ref, bands_ref):
    col = lax.axis_index("col")
    width = own.shape[0]
    for place in range(4):

        @pl.when(col == place)
        def _():
            for offset, block in enumerate((own, beside, across, diagonal)):
                lower = (place ^ offset) * width
                tokens_ref[:, lower : lower + width] = block[...].T

    fill_bands(kernel_ref, bands_ref)


def attention_kernel(
    latent_ref, tokens_ref, terms_own, terms_beside, terms_across, terms_diagonal, weight_ref,
    terms_ref, attended_ref, weight, weight_sem, normed, triple, mixed,
):
    fetch = pltpu.make_async_copy(weight_ref, weight, weight_sem)
    fetch.start()
    col = lax.axis_index("col")
    row = lax.axis_index("row")
    width = terms_own.shape[1]
    tiles = tokens_ref.shape[0] // TILE
    for place in range(4):

        @pl.when(col == place)
        def _():
            for offset, block in enumerate((terms_own, terms_beside, terms_across, terms_diagonal)):
                lower = (place ^ offset) * width
                terms_ref[:, lower : lower + width] = block[...]

    for tile in range(tiles):
        here = slice(tile * TILE, (tile + 1) * TILE)
        shift = tile_term(latent_ref, terms_ref, 0, tile)
        scale = tile_term(latent_ref, terms_ref, 1, tile)
        normed[here, :] = normalize(tokens_ref[here, :].astype(WIDE), shift, scale).astype(NARROW)
    fetch.wait()
    triple[...] = lax.dot_general(weight[...], normed[...], NT, preferred_element_type=WIDE)
    latents = [latent_ref[row * tiles + tile] for tile in range(tiles)]
    factor = HEAD_DIM ** (-0.5) * 1.4426950408889634
    pair = 2
    for head in range(width // HEAD_DIM):
        lower = head * HEAD_DIM
        queries = triple[lower : lower + HEAD_DIM, :].astype(NARROW)
        keys = triple[width + lower : width + lower + HEAD_DIM, :].T.astype(NARROW)
        values = triple[2 * width + lower : 2 * width + lower + HEAD_DIM, :]
        values = jnp.concatenate([values, jnp.ones((8, values.shape[1]), WIDE)]).astype(NARROW)
        for first in range(0, tiles, pair):
            here = slice(first * TILE, (first + pair) * TILE)
            scores = jnp.dot(keys, queries[:, here], preferred_element_type=WIDE)
            columns = []
            for tile in range(first, first + pair):
                lanes = slice((tile - first) * TILE, (tile - first + 1) * TILE)
                blocks = [
                    scores[other * TILE : (other + 1) * TILE, lanes]
                    + jnp.where(latents[other] == latents[tile], 0.0, -1e30)
                    for other in range(tiles)
                ]
                peak = functools.reduce(jnp.maximum, blocks)
                peak = jnp.max(peak, axis=0, keepdims=True)
                raised = [jnp.exp2((block - peak) * factor).astype(NARROW) for block in blocks]
                columns.append(jnp.concatenate(raised, axis=0))
            summed = jnp.dot(values, jnp.concatenate(columns, axis=1), preferred_element_type=WIDE)
            mixed[lower : lower + HEAD_DIM, here] = summed[:HEAD_DIM] / summed[HEAD_DIM : HEAD_DIM + 1]
    attended_ref[...] = mixed[...].T.astype(NARROW)


def stack_kernel(*refs):
    width = refs[0].shape[0]
    for offset, block in enumerate(refs[:-1]):
        refs[-1][offset * width : (offset + 1) * width, :] = block[...]


def weights_kernel(counts, depth, *refs):
    pieces, (expand, reduce) = list(refs[:-2]), refs[-2:]
    row = lax.axis_index("row")
    for offset, count in enumerate(counts):
        start = pl.multiple_of((row ^ offset) * depth, 16) if len(counts) > 1 else 0
        here = pl.ds(start, depth)
        if count == 1:
            both = pieces.pop(0)
            expand[here, :] = both[:depth, :]
            reduce[here, :] = both[depth:, :]
        else:
            expand[here, :] = pieces.pop(0)[...]
            reduce[here, :] = pieces.pop(0)[...]


def shared_kernel(parts_ref, head_ref, out_ref):
    count = parts_ref.shape[1]
    out_ref[:count, :] = jnp.sum(parts_ref[...], axis=0)
    out_ref[count:, :] = head_ref[...].astype(WIDE)


def mlp_kernel(
    near, latent_ref, att_own, att_beside, att_across, att_diagonal, tokens_ref, terms_ref, out_weight, expand, reduce, *refs
):
    outs, (attended, mid) = refs[:-2], refs[-2:]
    col = lax.axis_index("col")
    width = att_own.shape[1]
    tile_list = [col ^ offset for offset in ((0, 1) if near else (2, 3))]
    starts = [pl.multiple_of(tile * TILE, TILE) for tile in tile_list]
    for offset, block in enumerate((att_own, att_beside, att_across, att_diagonal)):
        for slot, start in enumerate(starts):
            here = slice(slot * TILE, (slot + 1) * TILE)
            attended[here, offset * width : (offset + 1) * width] = block[pl.ds(start, TILE), :]
    attn_sum = jnp.dot(attended[...], out_weight[...], preferred_element_type=WIDE)
    for slot, tile in enumerate(tile_list):
        term = functools.partial(tile_term, latent_ref, terms_ref, tile=tile)
        here = slice(slot * TILE, (slot + 1) * TILE)
        before = tokens_ref[pl.ds(starts[slot], TILE), :].astype(WIDE)
        residual = (before + term(2) * attn_sum[here]).astype(NARROW)
        if near and slot == 0:
            outs[2][...] = residual
        mid[here, :] = normalize(residual.astype(WIDE), term(3), term(4)).astype(NARROW)
    units = jnp.dot(mid[...], expand[...], preferred_element_type=WIDE)
    inner = 0.7978845608028654 * (units + 0.044715 * (units * units * units))
    activated = (0.5 * units * (1.0 + jnp.tanh(inner))).astype(NARROW)
    summed = lax.dot_general(activated, reduce[...], NT, preferred_element_type=WIDE)
    outs[0][...] = summed[:TILE]
    outs[1][...] = summed[TILE:].astype(NARROW)


def head_kernel(latent_ref, kept_ref, beside_ref, crossed_ref, residual_ref, terms_ref, out_ref):
    col = lax.axis_index("col")
    term = functools.partial(tile_term, latent_ref, terms_ref, tile=col)
    mlp_sum = kept_ref[...] + beside_ref[...].astype(WIDE) + crossed_ref[...].astype(WIDE)
    second = (residual_ref[...].astype(WIDE) + term(5) * mlp_sum).astype(NARROW).astype(WIDE)
    normed = normalize(second, term(6), term(7)).astype(NARROW)
    group = PATCH * CHANNELS
    token_place = lax.broadcasted_iota(jnp.int32, (TILE, IMG_WIDTH), 0) % GRIDW
    lane_place = lax.broadcasted_iota(jnp.int32, (TILE, IMG_WIDTH), 1) // group
    for dy in range(PATCH):
        rows = terms_ref[16 + dy * group : 16 + (dy + 1) * group, :].astype(NARROW)
        spread_rows = jnp.concatenate([rows.astype(WIDE)] * GRIDW, axis=0).astype(NARROW)
        noise = lax.dot_general(normed, spread_rows, NT, preferred_element_type=WIDE)
        noise = jnp.where(token_place == lane_place, noise, 0.0)
        folded = jnp.sum(noise.reshape(TILE_ROWS, GRIDW, IMG_WIDTH), axis=1)
        out_ref[:, dy * IMG_WIDTH : (dy + 1) * IMG_WIDTH] = folded


def fill_bands(kernel_ref, out_ref):
    shape = (IMG_WIDTH, IMG_WIDTH)
    source = lax.broadcasted_iota(jnp.int32, shape, 0)
    target = lax.broadcasted_iota(jnp.int32, shape, 1)
    reach = 3 * CHANNELS
    apart = target - (source // CHANNELS) * CHANNELS + CHANNELS
    code = jnp.where((apart >= 0) & (apart < reach), (source % CHANNELS) * reach + apart, -1)
    bands = [jnp.zeros(shape, WIDE) for _ in range(3)]
    for channel in range(CHANNELS):
        for lane in range(reach):
            here = code == channel * reach + lane
            column, out_channel = 2 - lane // CHANNELS, lane % CHANNELS
            for line in range(3):
                place = ((line * 3 + column) * CHANNELS + channel) * CHANNELS + out_channel
                bands[line] = jnp.where(here, kernel_ref[place], bands[line])
    for line in range(3):
        out_ref[:, line * IMG_WIDTH : (line + 1) * IMG_WIDTH] = bands[line]


def step_kernel(
    latent_ref, steps_ref, now_ref, next_ref, own, beside, across, diagonal, noisy_ref, bands_ref,
    stepped_ref, preview_ref, image, clean, above, below,
):
    tiles = noisy_ref.shape[0] // IMG_ROWS
    row = lax.axis_index("row")
    col = lax.axis_index("col")
    for place in range(4):

        @pl.when(col == place)
        def _():
            for offset, block in enumerate((own, beside, across, diagonal)):
                for dy in range(PATCH):
                    start = (place ^ offset) * IMG_ROWS + dy
                    image[pl.ds(start, TILE_ROWS, PATCH), :] = block[:, dy * IMG_WIDTH : (dy + 1) * IMG_WIDTH]

    for tile in range(tiles):
        here = slice(tile * IMG_ROWS, (tile + 1) * IMG_ROWS)
        step = steps_ref[latent_ref[row * tiles + tile]]
        signal_now = jnp.full((1, IMG_WIDTH), now_ref[step], WIDE)
        signal_next = jnp.full((1, IMG_WIDTH), next_ref[step], WIDE)
        noise = image[here, :]
        rows = (noisy_ref[here, :].astype(WIDE) - jnp.sqrt(1.0 - signal_now) * noise) / jnp.sqrt(signal_now)
        clean[here, :] = rows
        stepped = jnp.sqrt(signal_next) * rows + jnp.sqrt(1.0 - signal_next) * noise
        stepped_ref[here, :] = stepped.astype(NARROW)
    parts = jnp.dot(
        clean[...], bands_ref[...], precision=lax.Precision.HIGHEST, preferred_element_type=WIDE
    )
    count = tiles * IMG_ROWS
    above[8 : 8 + count, :] = parts[:, :IMG_WIDTH]
    below[8 : 8 + count, :] = parts[:, 2 * IMG_WIDTH :]
    for tile in range(tiles):
        here = slice(tile * IMG_ROWS, (tile + 1) * IMG_ROWS)
        start = 8 + tile * IMG_ROWS
        line = lax.broadcasted_iota(jnp.int32, (IMG_ROWS, IMG_WIDTH), 0)
        from_above = above[start - 1 : start - 1 + IMG_ROWS, :]
        from_below = below[start + 1 : start + 1 + IMG_ROWS, :]
        mine = latent_ref[row * tiles + tile]
        if tile == 0:
            above_ok = line > 0
        else:
            above_ok = (line > 0) | (latent_ref[row * tiles + tile - 1] == mine)
        if tile == tiles - 1:
            below_ok = line < IMG_ROWS - 1
        else:
            below_ok = (line < IMG_ROWS - 1) | (latent_ref[row * tiles + tile + 1] == mine)
        total = parts[here, IMG_WIDTH : 2 * IMG_WIDTH]
        total = total + jnp.where(above_ok, from_above, 0.0) + jnp.where(below_ok, from_below, 0.0)
        preview_ref[here, :] = total.astype(NARROW)


def shards(
    hidden,
    noisy_latent,
    tile_latent,
    timesteps,
    step_embedding,
    alpha_now,
    alpha_next,
    modulation,
    attention_in,
    attention_out,
    expand_weight,
    reduce_weight,
    noise_head,
    preview_kernel,
):
    rows = lax.axis_size("row")
    tokens_here, width = hidden.shape
    tiles = tokens_here // TILE
    depth = modulation.shape[0]
    units = expand_weight.shape[1]
    shape = jax.ShapeDtypeStruct

    conditioning = call(
        functools.partial(condition_kernel, tiles),
        shape((2 * rows, depth), NARROW),
        [SMEM, SMEM, VMEM],
        [pltpu.VMEM((2 * rows, STEPS), WIDE)],
        flops=2 * 2 * rows * D * (STEPS + depth), nbytes=2 * STEPS * D,
    )(tile_latent, timesteps, step_embedding)
    partial = jnp.einsum("td,dkc->tkc", conditioning, modulation, preferred_element_type=WIDE)
    partial = partial.reshape(rows, 16, width)
    received = lax.all_to_all(partial, "row", 0, 0, tiled=True)
    hidden_blocks = gather_blocks(hidden.T)
    out_rows = after(attention_out, hidden_blocks[2])
    pieces = gather_rows(expand_weight, reduce_weight.T)
    hidden_blocks = after(hidden_blocks, [piece for piece in pieces[:5] if piece is not pieces[3 % len(pieces)]])
    tokens, bands = call(
        tokens_kernel,
        [shape((tokens_here, D), NARROW), shape((IMG_WIDTH, 3 * IMG_WIDTH), WIDE)],
        [VMEM] * 4 + [SMEM],
        nbytes=4 * tokens_here * D, limit=8,
    )(*hidden_blocks, preview_kernel.reshape(-1))
    shared = call(shared_kernel, shape((32, width), WIDE), [VMEM] * 2, nbytes=2**18)(after(received, tokens), noise_head.T)
    shared_blocks = gather_blocks(shared)
    attention_weight = attention_in.transpose(1, 2, 0).reshape(3 * width, D)
    terms, attended = call(
        attention_kernel,
        [shape((32, D), WIDE), shape((tokens_here, width), NARROW)],
        [SMEM] + [VMEM] * 5 + [ANYWHERE],
        [
            pltpu.VMEM((3 * width, D), NARROW),
            pltpu.SemaphoreType.DMA,
            pltpu.VMEM((tokens_here, D), NARROW),
            pltpu.VMEM((3 * width, tokens_here), WIDE),
            pltpu.VMEM((width, tokens_here), WIDE),
        ],
        flops=2 * tokens_here * (D * 3 * width + 2 * tokens_here * width), nbytes=5 * 2**20,
        trans=4 * tokens_here**2, limit=24,
    )(tile_latent, tokens, *shared_blocks, attention_weight)
    out_blocks = gather_late(out_rows, attended)
    attended_blocks = gather_blocks(attended)

    out_weight = call(
        stack_kernel, shape((D, D), NARROW), [VMEM] * 4, nbytes=4 * D * D, limit=8
    )(*out_blocks)
    expand_all, reduce_all = call(
        functools.partial(weights_kernel, [len(piece) for piece in pieces], D // len(pieces)),
        [shape((D, units), NARROW)] * 2, [VMEM] * sum(map(len, pieces)), nbytes=8 * D * units, limit=8,
    )(*sum(pieces, []))
    def mlp(near, inputs):
        outs = [shape((TILE, D), WIDE), shape((TILE, D), NARROW)]
        if near:
            outs.append(shape((TILE, D), NARROW))
        return call(
            functools.partial(mlp_kernel, near),
            outs,
            [SMEM] + [VMEM] * 9,
            [pltpu.VMEM((2 * TILE, D), NARROW)] * 2,
            flops=4 * TILE * D * (D + 2 * units), nbytes=8 * 2**20, trans=2 * TILE * units, limit=20,
        )(tile_latent, *inputs, out_weight, expand_all, reduce_all)

    inputs = (*attended_blocks, tokens, terms)
    far_kept, far_sent = mlp(False, inputs)
    far_sum = (far_kept + exchange(far_sent, "col", 1).astype(WIDE)).astype(NARROW)
    far_sum, inputs = lax.optimization_barrier((far_sum, inputs))
    crossed = exchange(far_sum, "col", 2)
    near_kept, near_sent, residual = mlp(True, inputs)
    near_sent, crossed, bands = lax.optimization_barrier((near_sent, crossed, bands))
    beside = exchange(near_sent, "col", 1)
    noise = call(
        head_kernel,
        shape((TILE_ROWS, PATCH * IMG_WIDTH), WIDE),
        [SMEM] + [VMEM] * 5,
        flops=4 * TILE * D * IMG_WIDTH, nbytes=2**21, limit=8,
    )(tile_latent, near_kept, beside, crossed, residual, terms)

    img_rows = tiles * IMG_ROWS
    stepped, preview = call(
        step_kernel,
        [shape((img_rows, IMG_WIDTH), NARROW)] * 2,
        [SMEM] * 4 + [VMEM] * 6,
        [pltpu.VMEM((img_rows, IMG_WIDTH), WIDE)] * 2
        + [pltpu.VMEM((img_rows + 16, IMG_WIDTH), WIDE)] * 2,
        flops=12 * img_rows * IMG_WIDTH**2, nbytes=2**19,
    )(tile_latent, timesteps, alpha_now, alpha_next, *gather_blocks(noise), noisy_latent, bands)
    return (stepped, preview)


def solution(mesh):
    return jax.shard_map(
        shards,
        mesh=mesh,
        in_specs=(
            P("row", "col"),
            P("row", None),
            P(),
            P(),
            P(),
            P(),
            P(),
            P("row", None, "col"),
            P(None, None, "col"),
            P("col", None),
            P("row", "col"),
            P("col", "row"),
            P("col", None),
            P(),
        ),
        out_specs=(P("row", None), P("row", None)),
        check_vma=False,
    )
```

```python
import functools

import jax
import jax.numpy as jnp
from jax import lax
from jax.experimental import pallas as pl
from jax.experimental.pallas import tpu as pltpu
from jax.sharding import PartitionSpec as P

D = 1152
HEAD_DIM = 72
PATCH = 2
CHANNELS = 4
GRIDW = 16
TILE_ROWS = 8
STEPS = 50
TILE = 128
EPS_NORM = 1e-06
IMG_ROWS = TILE_ROWS * PATCH
IMG_WIDTH = GRIDW * PATCH * CHANNELS
WIDE = jnp.float32
NARROW = jnp.bfloat16
NT = (((1,), (1,)), ((), ()))
VMEM = pl.BlockSpec(memory_space=pltpu.VMEM)
SMEM = pl.BlockSpec(memory_space=pltpu.SMEM)
ANYWHERE = pl.BlockSpec(memory_space=pl.ANY)
MIB = 1024 * 1024


def call(kernel, outs, in_specs, scratch=(), flops=0, nbytes=0, trans=0, limit=4):
    return pl.pallas_call(
        kernel,
        out_shape=outs,
        in_specs=in_specs,
        out_specs=jax.tree.map(lambda _: VMEM, outs),
        scratch_shapes=list(scratch),
        compiler_params=pltpu.CompilerParams(vmem_limit_bytes=limit * MIB),
        cost_estimate=pl.CostEstimate(flops=flops, bytes_accessed=nbytes, transcendentals=trans),
    )


def exchange(value, axis, offset):
    size = lax.axis_size(axis)
    return lax.ppermute(value, axis, [(i, i ^ offset) for i in range(size)])


def gather_blocks(value):
    across = exchange(value, "col", 2)
    beside = exchange(value, "col", 1)
    diagonal = exchange(across, "col", 1)
    return value, beside, across, diagonal


def pack(first, second, *before):
    out = jax.ShapeDtypeStruct((2 * first.shape[0], first.shape[1]), first.dtype)
    return call(pair_kernel, out, [VMEM] * 2 + [ANYWHERE] * len(before), limit=8)(first, second, *before)


def normalize(values, shift_term, scale_term):
    mean_value = jnp.sum(values, axis=-1, keepdims=True) * (1.0 / D)
    spread = jnp.sum(values * values, axis=-1, keepdims=True) * (1.0 / D) - mean_value * mean_value
    normed = (values - mean_value) * lax.rsqrt(spread + EPS_NORM)
    return normed * (1.0 + scale_term) + shift_term


def condition_kernel(tiles_here, table_ref, embedding_ref, out_ref, mark_ref, onehot):
    count, depth = out_ref.shape
    tile_count = count // 2 * tiles_here
    mark_ref[...] = jnp.zeros(mark_ref.shape, WIDE)

    def pick(index, carry):
        tile = (index // 2) * tiles_here + (index % 2) * (tiles_here - 1)
        step = table_ref[tile_count + table_ref[tile]]
        lanes = lax.broadcasted_iota(jnp.int32, (1, STEPS), 1)
        onehot[pl.ds(index, 1), :] = jnp.where(lanes == step, 1.0, 0.0)
        return carry

    lax.fori_loop(0, count, pick, 0)
    embedded = jnp.dot(onehot[...].astype(NARROW), embedding_ref[...], preferred_element_type=WIDE)
    conditioning = (embedded / (1.0 + jnp.exp(-embedded))).astype(NARROW)
    first = lax.axis_index("row") * depth
    source = lax.broadcasted_iota(jnp.int32, (D, depth), 0)
    target = lax.broadcasted_iota(jnp.int32, (D, depth), 1) + first
    chosen = jnp.where(source == target, 1.0, 0.0).astype(NARROW)
    out_ref[...] = jnp.dot(conditioning, chosen, preferred_element_type=WIDE).astype(NARROW)


def tile_term(latent_ref, terms_ref, index, tile):
    first = lax.axis_index("row") * (lax.axis_size("col"))
    later = latent_ref[first + tile] != latent_ref[first]
    return jnp.where(later, terms_ref[8 + index : 9 + index, :], terms_ref[index : index + 1, :])


def pass_kernel(*refs):
    refs[-1][...] = refs[0][...]


def triple_kernel(
    latent_ref, own, beside, across, diagonal, terms_near, terms_far, weight_ref, *refs
):
    tokens_ref, terms_ref, triple_ref, weight, weight_sem, normed = refs[-6:]
    fetch = pltpu.make_async_copy(weight_ref, weight, weight_sem)
    fetch.start()
    col = lax.axis_index("col")
    width = terms_near.shape[1]
    tiles = tokens_ref.shape[0] // TILE
    for place in range(4):

        @pl.when(col == place)
        def _():
            for offset, block in enumerate((own, beside, across, diagonal)):
                lower = (place ^ offset) * width
                tokens_ref[:, lower : lower + width] = block[...].T
            for offset in range(4):
                block = (terms_near, terms_far)[offset // 2]
                lower = (place ^ offset) * width
                count = terms_ref.shape[0]
                terms_ref[:, lower : lower + width] = block[offset % 2 * count : (offset % 2 + 1) * count, :]

    for tile in range(tiles):
        here = slice(tile * TILE, (tile + 1) * TILE)
        shift = tile_term(latent_ref, terms_ref, 0, tile)
        scale = tile_term(latent_ref, terms_ref, 1, tile)
        normed[here, :] = normalize(tokens_ref[here, :].astype(WIDE), shift, scale).astype(NARROW)
    fetch.wait()
    triple_ref[...] = lax.dot_general(weight[...], normed[...], NT, preferred_element_type=WIDE)


def attention_kernel(latent_ref, triple, *refs):
    attended_ref, mark_ref, mixed = refs[-3:]
    mark_ref[...] = jnp.zeros(mark_ref.shape, WIDE)
    row = lax.axis_index("row")
    width = attended_ref.shape[1]
    tiles = attended_ref.shape[0] // TILE
    latents = [latent_ref[row * tiles + tile] for tile in range(tiles)]
    factor = HEAD_DIM ** (-0.5) * 1.4426950408889634
    pair = 2
    for head in range(width // HEAD_DIM):
        lower = head * HEAD_DIM
        queries = triple[lower : lower + HEAD_DIM, :].astype(NARROW)
        keys = triple[width + lower : width + lower + HEAD_DIM, :].T.astype(NARROW)
        values = triple[2 * width + lower : 2 * width + lower + HEAD_DIM, :]
        values = jnp.concatenate([values, jnp.ones((8, values.shape[1]), WIDE)]).astype(NARROW)
        for first in range(0, tiles, pair):
            here = slice(first * TILE, (first + pair) * TILE)
            scores = jnp.dot(keys, queries[:, here], preferred_element_type=WIDE)
            columns = []
            for tile in range(first, first + pair):
                lanes = slice((tile - first) * TILE, (tile - first + 1) * TILE)
                blocks = [
                    scores[other * TILE : (other + 1) * TILE, lanes]
                    + jnp.where(latents[other] == latents[tile], 0.0, -1e30)
                    for other in range(tiles)
                ]
                peak = functools.reduce(jnp.maximum, blocks)
                peak = jnp.max(peak, axis=0, keepdims=True)
                raised = [jnp.exp2((block - peak) * factor).astype(NARROW) for block in blocks]
                columns.append(jnp.concatenate(raised, axis=0))
            summed = jnp.dot(values, jnp.concatenate(columns, axis=1), preferred_element_type=WIDE)
            mixed[lower : lower + HEAD_DIM, here] = summed[:HEAD_DIM] / summed[HEAD_DIM : HEAD_DIM + 1]
    attended_ref[...] = mixed[...].T.astype(NARROW)


def stack_kernel(near, far, kernel_ref, out_ref, bands_ref):
    width = near.shape[0]
    out_ref[:width, :] = near[...]
    out_ref[width:, :] = far[...]
    fill_bands(kernel_ref, bands_ref)


def weights_kernel(parts, depth, whole, *refs):
    pieces, (expand, reduce) = list(refs[: len(parts) + 2 * whole]), refs[-2:]
    row = lax.axis_index("row")
    if whole:
        expand[...] = pieces.pop(0)[...]
        reduce[...] = pieces.pop(0)[...]
    for (offset, which), piece in zip(parts, pieces):
        start = pl.multiple_of((row ^ offset) * depth, 16) if depth < D else 0
        here = pl.ds(start, depth)
        if "e" in which:
            expand[here, :] = piece[:depth, :]
        if "r" in which:
            reduce[here, :] = piece[-depth:, :]


def pair_kernel(first, second, *refs):
    out_ref = refs[-1]
    count = first.shape[0]
    out_ref[:count, :] = first[...]
    out_ref[count:, :] = second[...]


def order_kernel(*refs):
    refs[-1][...] = jnp.zeros(refs[-1].shape, WIDE)


def shared_kernel(parts_ref, head_ref, _, out_ref, mark_ref):
    count = parts_ref.shape[1]
    out_ref[:count, :] = jnp.sum(parts_ref[...], axis=0)
    out_ref[count:, :] = head_ref[...].astype(WIDE)
    mark_ref[...] = jnp.zeros(mark_ref.shape, WIDE)


def mlp_kernel(
    offsets, latent_ref, att_own, att_across, att_beside, att_diagonal, tokens_ref, terms_ref, out_weight, expand, reduce, *refs
):
    outs, (mark_ref, attended, mid) = refs[-3 - len(offsets) - (0 in offsets) : -3], refs[-3:]
    mark_ref[...] = jnp.zeros(mark_ref.shape, WIDE)
    col = lax.axis_index("col")
    width = att_own.shape[1]
    tile_list = [col ^ offset for offset in offsets]
    starts = [pl.multiple_of(tile * TILE, TILE) for tile in tile_list]
    for place, block in enumerate((att_own, att_across, att_beside, att_diagonal)):
        for slot, start in enumerate(starts):
            here = slice(slot * TILE, (slot + 1) * TILE)
            attended[here, place * width : (place + 1) * width] = block[pl.ds(start, TILE), :]
    attn_sum = jnp.dot(attended[...], out_weight[...], preferred_element_type=WIDE)
    for slot, tile in enumerate(tile_list):
        term = functools.partial(tile_term, latent_ref, terms_ref, tile=tile)
        here = slice(slot * TILE, (slot + 1) * TILE)
        before = tokens_ref[pl.ds(starts[slot], TILE), :].astype(WIDE)
        residual = (before + term(2) * attn_sum[here]).astype(NARROW)
        if offsets[slot] == 0:
            outs[-1][...] = residual
        mid[here, :] = normalize(residual.astype(WIDE), term(3), term(4)).astype(NARROW)
    units = jnp.dot(mid[...], expand[...], preferred_element_type=WIDE)
    inner = 0.7978845608028654 * (units + 0.044715 * (units * units * units))
    activated = (0.5 * units * (1.0 + jnp.tanh(inner))).astype(NARROW)
    summed = lax.dot_general(activated, reduce[...], NT, preferred_element_type=WIDE)
    for slot, out in enumerate(outs[: len(offsets)]):
        out[...] = summed[slot * TILE : (slot + 1) * TILE].astype(out.dtype)


def head_kernel(latent_ref, kept_ref, beside_ref, crossed_ref, residual_ref, terms_ref, out_ref):
    col = lax.axis_index("col")
    term = functools.partial(tile_term, latent_ref, terms_ref, tile=col)
    mlp_sum = kept_ref[...] + beside_ref[...].astype(WIDE) + crossed_ref[...].astype(WIDE)
    second = (residual_ref[...].astype(WIDE) + term(5) * mlp_sum).astype(NARROW).astype(WIDE)
    normed = normalize(second, term(6), term(7)).astype(NARROW)
    group = PATCH * CHANNELS
    token_place = lax.broadcasted_iota(jnp.int32, (TILE, IMG_WIDTH), 0) % GRIDW
    lane_place = lax.broadcasted_iota(jnp.int32, (TILE, IMG_WIDTH), 1) // group
    for dy in range(PATCH):
        rows = terms_ref[16 + dy * group : 16 + (dy + 1) * group, :].astype(NARROW)
        spread_rows = jnp.concatenate([rows.astype(WIDE)] * GRIDW, axis=0).astype(NARROW)
        noise = lax.dot_general(normed, spread_rows, NT, preferred_element_type=WIDE)
        noise = jnp.where(token_place == lane_place, noise, 0.0)
        folded = jnp.sum(noise.reshape(TILE_ROWS, GRIDW, IMG_WIDTH), axis=1)
        out_ref[:, dy * IMG_WIDTH : (dy + 1) * IMG_WIDTH] = folded


def fill_bands(kernel_ref, out_ref):
    shape = (IMG_WIDTH, IMG_WIDTH)
    source = lax.broadcasted_iota(jnp.int32, shape, 0)
    target = lax.broadcasted_iota(jnp.int32, shape, 1)
    reach = 3 * CHANNELS
    apart = target - (source // CHANNELS) * CHANNELS + CHANNELS
    code = jnp.where((apart >= 0) & (apart < reach), (source % CHANNELS) * reach + apart, -1)
    bands = [jnp.zeros(shape, WIDE) for _ in range(3)]
    for channel in range(CHANNELS):
        for lane in range(reach):
            here = code == channel * reach + lane
            column, out_channel = 2 - lane // CHANNELS, lane % CHANNELS
            for line in range(3):
                value = kernel_ref[line, column, channel, out_channel]
                bands[line] = jnp.where(here, value, bands[line])
    for line in range(3):
        out_ref[:, line * IMG_WIDTH : (line + 1) * IMG_WIDTH] = bands[line]


def step_kernel(
    table_ref, now_ref, next_ref, near, far, noisy_ref, bands_ref,
    stepped_ref, preview_ref, image, clean, above, below,
):
    tiles = noisy_ref.shape[0] // IMG_ROWS
    row = lax.axis_index("row")
    tile_count = lax.axis_size("row") * tiles
    col = lax.axis_index("col")
    for place in range(4):

        @pl.when(col == place)
        def _():
            for offset in range(4):
                block = (near, far)[offset // 2]
                rows = slice(offset % 2 * TILE_ROWS, (offset % 2 + 1) * TILE_ROWS)
                for dy in range(PATCH):
                    start = (place ^ offset) * IMG_ROWS + dy
                    image[pl.ds(start, TILE_ROWS, PATCH), :] = block[rows, dy * IMG_WIDTH : (dy + 1) * IMG_WIDTH]

    for tile in range(tiles):
        here = slice(tile * IMG_ROWS, (tile + 1) * IMG_ROWS)
        step = table_ref[tile_count + table_ref[row * tiles + tile]]
        signal_now = jnp.full((1, IMG_WIDTH), now_ref[step], WIDE)
        signal_next = jnp.full((1, IMG_WIDTH), next_ref[step], WIDE)
        noise = image[here, :]
        rows = (noisy_ref[here, :].astype(WIDE) - jnp.sqrt(1.0 - signal_now) * noise) / jnp.sqrt(signal_now)
        clean[here, :] = rows
        stepped = jnp.sqrt(signal_next) * rows + jnp.sqrt(1.0 - signal_next) * noise
        stepped_ref[here, :] = stepped.astype(NARROW)
    parts = jnp.dot(
        clean[...], bands_ref[...], precision=lax.Precision.HIGHEST, preferred_element_type=WIDE
    )
    count = tiles * IMG_ROWS
    above[8 : 8 + count, :] = parts[:, :IMG_WIDTH]
    below[8 : 8 + count, :] = parts[:, 2 * IMG_WIDTH :]
    for tile in range(tiles):
        here = slice(tile * IMG_ROWS, (tile + 1) * IMG_ROWS)
        start = 8 + tile * IMG_ROWS
        line = lax.broadcasted_iota(jnp.int32, (IMG_ROWS, IMG_WIDTH), 0)
        from_above = above[start - 1 : start - 1 + IMG_ROWS, :]
        from_below = below[start + 1 : start + 1 + IMG_ROWS, :]
        mine = table_ref[row * tiles + tile]
        if tile == 0:
            above_ok = line > 0
        else:
            above_ok = (line > 0) | (table_ref[row * tiles + tile - 1] == mine)
        if tile == tiles - 1:
            below_ok = line < IMG_ROWS - 1
        else:
            below_ok = (line < IMG_ROWS - 1) | (table_ref[row * tiles + tile + 1] == mine)
        total = parts[here, IMG_WIDTH : 2 * IMG_WIDTH]
        total = total + jnp.where(above_ok, from_above, 0.0) + jnp.where(below_ok, from_below, 0.0)
        preview_ref[here, :] = total.astype(NARROW)


def shards(
    hidden,
    noisy_latent,
    tile_latent,
    timesteps,
    step_embedding,
    alpha_now,
    alpha_next,
    modulation,
    attention_in,
    attention_out,
    expand_weight,
    reduce_weight,
    noise_head,
    preview_kernel,
):
    rows = lax.axis_size("row")
    tokens_here, width = hidden.shape
    tiles = tokens_here // TILE
    depth = modulation.shape[0]
    units = expand_weight.shape[1]
    shape = jax.ShapeDtypeStruct

    table = jnp.concatenate([tile_latent, timesteps])
    mark = shape((8, 128), WIDE)
    conditioning, conditioned = call(
        functools.partial(condition_kernel, tiles),
        [shape((2 * rows, depth), NARROW), mark],
        [SMEM, VMEM],
        [pltpu.VMEM((2 * rows, STEPS), WIDE)],
        flops=2 * 2 * rows * D * (STEPS + depth), nbytes=2 * STEPS * D,
    )(table, step_embedding)
    partial = jnp.einsum("td,dkc->tkc", conditioning, modulation, preferred_element_type=WIDE)
    partial = partial.reshape(rows, 16, width)
    received = lax.all_to_all(partial, "row", 0, 0, tiled=True)
    hidden_blocks = gather_blocks(hidden.T)
    out_rows, conditioned = lax.optimization_barrier((attention_out, conditioned))
    reduce_rows = reduce_weight.T
    staged = rows == 8
    if staged:
        both = jnp.concatenate([expand_weight, reduce_rows], axis=0)
        both_4 = exchange(both, "row", 4)
        both_2 = exchange(both, "row", 2)
        both_1 = exchange(both, "row", 1)
        first, middle = [both_4, both_2, both_1], []
    else:
        expand_whole = lax.all_gather(expand_weight, "row", axis=0, tiled=True)
        reduce_whole = lax.all_gather(reduce_rows, "row", axis=0, tiled=True)
        first, middle = [], []
    arrived = call(order_kernel, mark, [ANYWHERE] * (3 + len(first)))(conditioned, *hidden_blocks[1::2], *first)
    shared, shared_done = call(
        shared_kernel, [shape((32, width), WIDE), mark], [VMEM] * 2 + [ANYWHERE], nbytes=2**18
    )(received, noise_head.T, arrived)
    terms_near = pack(shared, exchange(shared, "col", 1), *middle)
    terms_far = exchange(terms_near, "col", 2)
    second, third = [], []
    if staged:
        both_3 = exchange(both_2, "row", 1)
        both_6 = exchange(both_4, "row", 2)
        both_5 = exchange(both_4, "row", 1)
        both_7 = exchange(both_6, "row", 1)
        second = [both_3, both_6]
        third = [both_5]
        parts = [(i, "er", piece) for i, piece in enumerate((both, both_1, both_2, both_3, both_4, both_5, both_6))]
        last = [(7, "er", both_7)]
    else:
        parts, last = [(0, "e", expand_whole), (0, "r", reduce_whole)], []
    attention_weight = attention_in.transpose(1, 2, 0).reshape(3 * width, D)
    tokens, terms, triple = call(
        triple_kernel,
        [shape((tokens_here, D), NARROW), shape((32, D), WIDE), shape((3 * width, tokens_here), WIDE)],
        [SMEM] + [VMEM] * 6 + [ANYWHERE] * (1 + len(second)),
        [
            pltpu.VMEM((3 * width, D), NARROW),
            pltpu.SemaphoreType.DMA,
            pltpu.VMEM((tokens_here, D), NARROW),
        ],
        flops=2 * tokens_here * D * 3 * width, nbytes=5 * 2**20, limit=16,
    )(table, *hidden_blocks, terms_near, terms_far, attention_weight, *second)
    attended, attention_done = call(
        attention_kernel,
        [shape((tokens_here, width), NARROW), mark],
        [SMEM, VMEM] + [ANYWHERE] * len(third),
        [pltpu.VMEM((width, tokens_here), WIDE)],
        flops=4 * tokens_here * tokens_here * width, trans=4 * tokens_here**2, limit=16,
    )(table, triple, *third)
    out_near = pack(out_rows, exchange(out_rows, "col", 2), attention_done)
    out_weight, bands = call(
        stack_kernel,
        [shape((D, D), NARROW), shape((IMG_WIDTH, 3 * IMG_WIDTH), WIDE)],
        [VMEM] * 2 + [SMEM], nbytes=4 * D * D, limit=8,
    )(out_near, exchange(out_near, "col", 1), preview_kernel)
    weights = ()
    for group in (parts, last):
        if group:
            weights = call(
                functools.partial(
                    weights_kernel, [part[:2] for part in group], depth if staged else D, len(weights) > 0
                ),
                [shape((D, units), NARROW)] * 2, [VMEM] * (len(weights) + len(group)), nbytes=8 * D * units, limit=8,
            )(*weights, *(part[2] for part in group))
        if group is parts:
            across = exchange(attended, "col", 2)
            passed = call(
                pass_kernel, shape(across.shape, NARROW), [VMEM] + [ANYWHERE] * 2, nbytes=2**19
            )(across, out_weight, weights[0])
            attended_blocks = (attended, across, exchange(attended, "col", 1), exchange(passed, "col", 1))
    expand_all, reduce_all = weights

    def mlp(offsets, *before):
        outs = [shape((TILE, D), NARROW if offset % 2 else WIDE) for offset in offsets]
        if 0 in offsets:
            outs.append(shape((TILE, D), NARROW))
        outs.append(mark)
        count = len(offsets) * TILE
        return call(
            functools.partial(mlp_kernel, offsets),
            outs,
            [SMEM] + [VMEM] * 9 + [ANYWHERE] * len(before),
            [pltpu.VMEM((count, D), NARROW)] * 2,
            flops=2 * count * D * (D + 2 * units), nbytes=8 * 2**20, trans=count * units, limit=20,
        )(table, *attended_blocks, tokens, terms, out_weight, expand_all, reduce_all, *before)

    far_kept, far_sent, far_done = mlp((2, 3))
    near_sent, _ = mlp((1,), far_done)
    far_sum = (far_kept + exchange(far_sent, "col", 1).astype(WIDE)).astype(NARROW)
    crossed = exchange(far_sum, "col", 2)
    beside = exchange(near_sent, "col", 1)
    near_kept, residual, _ = mlp((0,), far_sum)
    noise = call(
        head_kernel,
        shape((TILE_ROWS, PATCH * IMG_WIDTH), WIDE),
        [SMEM] + [VMEM] * 5,
        flops=4 * TILE * D * IMG_WIDTH, nbytes=2**21, limit=8,
    )(table, near_kept, beside, crossed, residual, terms)

    noise_near = pack(noise, exchange(noise, "col", 1))
    img_rows = tiles * IMG_ROWS
    stepped, preview = call(
        step_kernel,
        [shape((img_rows, IMG_WIDTH), NARROW)] * 2,
        [SMEM] * 3 + [VMEM] * 4,
        [pltpu.VMEM((img_rows, IMG_WIDTH), WIDE)] * 2
        + [pltpu.VMEM((img_rows + 16, IMG_WIDTH), WIDE)] * 2,
        flops=12 * img_rows * IMG_WIDTH**2, nbytes=2**19,
    )(table, alpha_now, alpha_next, noise_near, exchange(noise_near, "col", 2), noisy_latent, bands)
    return (stepped, preview)


def solution(mesh):
    return jax.shard_map(
        shards,
        mesh=mesh,
        in_specs=(
            P("row", "col"),
            P("row", None),
            P(),
            P(),
            P(),
            P(),
            P(),
            P("row", None, "col"),
            P(None, None, "col"),
            P("col", None),
            P("row", "col"),
            P("col", "row"),
            P("col", None),
            P(),
        ),
        out_specs=(P("row", None), P("row", None)),
        check_vma=False,
    )
```

```python
import functools

import jax
import jax.numpy as jnp
from jax import lax
from jax.experimental import pallas as pl
from jax.experimental.pallas import tpu as pltpu
from jax.sharding import PartitionSpec as P

D = 1152
HEAD_DIM = 72
PATCH = 2
CHANNELS = 4
GRIDW = 16
F = {'p3': 2, 'p6': 2, 'p5': 0}
COSTS = {}
COUNT = [0]
TILE_ROWS = 8
STEPS = 50
TILE = 128
EPS_NORM = 1e-06
IMG_ROWS = TILE_ROWS * PATCH
IMG_WIDTH = GRIDW * PATCH * CHANNELS
WIDE = jnp.float32
NARROW = jnp.bfloat16
NT = (((1,), (1,)), ((), ()))
VMEM = pl.BlockSpec(memory_space=pltpu.VMEM)
SMEM = pl.BlockSpec(memory_space=pltpu.SMEM)
ANYWHERE = pl.BlockSpec(memory_space=pl.ANY)
MIB = 1024 * 1024


def call(kernel, outs, in_specs, scratch=(), flops=0, nbytes=0, trans=0, limit=4):
    base = getattr(kernel, "func", kernel).__name__
    COUNT[0] += 1
    if base in COSTS:
        flops, nbytes, trans = int(COSTS[base] * 10**9), 0, 0
    return pl.pallas_call(
        kernel,
        out_shape=outs,
        in_specs=in_specs,
        out_specs=jax.tree.map(lambda _: VMEM, outs),
        scratch_shapes=list(scratch),
        compiler_params=pltpu.CompilerParams(vmem_limit_bytes=limit * MIB),
        cost_estimate=pl.CostEstimate(flops=flops, bytes_accessed=nbytes, transcendentals=trans),
    )


def exchange(value, axis, offset):
    size = lax.axis_size(axis)
    return lax.ppermute(value, axis, [(i, i ^ offset) for i in range(size)])


def gather_blocks(value):
    across = exchange(value, "col", 2)
    beside = exchange(value, "col", 1)
    diagonal = exchange(across, "col", 1)
    return value, beside, across, diagonal


def pack(first, second, *before):
    out = jax.ShapeDtypeStruct((2 * first.shape[0], first.shape[1]), first.dtype)
    return call(pair_kernel, out, [VMEM] * 2 + [ANYWHERE] * len(before), limit=8)(first, second, *before)


def normalize(values, shift_term, scale_term):
    mean_value = jnp.sum(values, axis=-1, keepdims=True) * (1.0 / D)
    spread = jnp.sum(values * values, axis=-1, keepdims=True) * (1.0 / D) - mean_value * mean_value
    normed = (values - mean_value) * lax.rsqrt(spread + EPS_NORM)
    return normed * (1.0 + scale_term) + shift_term


def condition_kernel(tiles_here, table_ref, embedding_ref, out_ref, mark_ref, onehot):
    count, depth = out_ref.shape
    tile_count = count // 2 * tiles_here
    mark_ref[...] = jnp.zeros(mark_ref.shape, WIDE)

    def pick(index, carry):
        tile = (index // 2) * tiles_here + (index % 2) * (tiles_here - 1)
        step = table_ref[tile_count + table_ref[tile]]
        lanes = lax.broadcasted_iota(jnp.int32, (1, STEPS), 1)
        onehot[pl.ds(index, 1), :] = jnp.where(lanes == step, 1.0, 0.0)
        return carry

    lax.fori_loop(0, count, pick, 0)
    embedded = jnp.dot(onehot[...].astype(NARROW), embedding_ref[...], preferred_element_type=WIDE)
    conditioning = (embedded / (1.0 + jnp.exp(-embedded))).astype(NARROW)
    first = lax.axis_index("row") * depth
    source = lax.broadcasted_iota(jnp.int32, (D, depth), 0)
    target = lax.broadcasted_iota(jnp.int32, (D, depth), 1) + first
    chosen = jnp.where(source == target, 1.0, 0.0).astype(NARROW)
    out_ref[...] = jnp.dot(conditioning, chosen, preferred_element_type=WIDE).astype(NARROW)


def tile_term(latent_ref, terms_ref, index, tile):
    first = lax.axis_index("row") * (lax.axis_size("col"))
    later = latent_ref[first + tile] != latent_ref[first]
    return jnp.where(later, terms_ref[8 + index : 9 + index, :], terms_ref[index : index + 1, :])


def pass_kernel(*refs):
    refs[-1][...] = refs[0][...]


def terms_kernel(terms_near, terms_far, terms_ref, columns):
    col = lax.axis_index("col")
    width = terms_near.shape[1]
    rows = terms_ref.shape[0]
    for place in range(4):

        @pl.when(col == place)
        def _():
            for offset in range(4):
                block = (terms_near, terms_far)[offset // 2]
                lower = (place ^ offset) * width
                terms_ref[:, lower : lower + width] = block[offset % 2 * rows : (offset % 2 + 1) * rows, :]

    columns[...] = terms_ref[...].T


def triple_kernel(latent_ref, near, far, columns, weight_ref, *refs):
    triple_ref, weight, weight_sem, normed = refs[-4:]
    fetch = pltpu.make_async_copy(weight_ref, weight, weight_sem)
    fetch.start()
    col = lax.axis_index("col")
    width, count = near.shape[0] // 2, triple_ref.shape[1]
    blocks = [source[pl.ds(half * width, width), :count] for half in (0, 1) for source in (near, far)]
    total = jnp.zeros((1, count), WIDE)
    squares = jnp.zeros((1, count), WIDE)
    for block in blocks:
        values = block.astype(WIDE)
        total = total + jnp.sum(values, axis=0, keepdims=True)
        squares = squares + jnp.sum(values * values, axis=0, keepdims=True)
    mean_value = total * (1.0 / D)
    spread = squares * (1.0 / D) - mean_value * mean_value
    rate = lax.rsqrt(spread + EPS_NORM)
    first = lax.axis_index("row") * (count // TILE)
    later = [latent_ref[first + tile] != latent_ref[first] for tile in range(count // TILE)]
    for offset, block in enumerate(blocks):
        here = pl.ds(pl.multiple_of((col ^ offset) * width, 32), width)
        shifts = [jnp.broadcast_to(columns[here, at : at + 1], (width, TILE)) for at in (0, 8)]
        scales = [jnp.broadcast_to(columns[here, at : at + 1], (width, TILE)) + 1.0 for at in (1, 9)]
        for tile in range(count // TILE):
            lanes = slice(tile * TILE, (tile + 1) * TILE)
            values = (block[:, lanes].astype(WIDE) - mean_value[:, lanes]) * rate[:, lanes]
            scale = jnp.where(later[tile], scales[1], scales[0])
            shift = jnp.where(later[tile], shifts[1], shifts[0])
            normed[here, lanes] = (values * scale + shift).astype(NARROW)
    fetch.wait()
    triple_ref[...] = jnp.dot(weight[...], normed[...], preferred_element_type=WIDE)


def assemble_kernel(parts, depth, kernel_ref, near, far, *refs):
    pieces, (out_weight, expand, reduce, tokens_ref, bands_ref) = refs[: len(parts)], refs[-5:]
    col = lax.axis_index("col")
    width, count = near.shape[0] // 2, tokens_ref.shape[0]
    out_weight[: 2 * width, :] = near[:, count:]
    out_weight[2 * width :, :] = far[:, count:]
    place_pieces(parts, depth, pieces, expand, reduce)
    for place in range(4):

        @pl.when(col == place)
        def _():
            for offset in range(4):
                lower = (place ^ offset) * width
                source = (near, far)[offset % 2]
                tokens_ref[:, lower : lower + width] = source[pl.ds(offset // 2 * width, width), :count].T

    fill_bands(kernel_ref, bands_ref)


def attention_kernel(latent_ref, triple, *refs):
    attended_ref, mark_ref, mixed = refs[-3:]
    mark_ref[...] = jnp.zeros(mark_ref.shape, WIDE)
    row = lax.axis_index("row")
    width = attended_ref.shape[1]
    tiles = attended_ref.shape[0] // TILE
    latents = [latent_ref[row * tiles + tile] for tile in range(tiles)]
    factor = HEAD_DIM ** (-0.5) * 1.4426950408889634
    pair = 2
    for head in range(width // HEAD_DIM):
        lower = head * HEAD_DIM
        queries = triple[lower : lower + HEAD_DIM, :].astype(NARROW)
        keys = triple[width + lower : width + lower + HEAD_DIM, :].T.astype(NARROW)
        values = triple[2 * width + lower : 2 * width + lower + HEAD_DIM, :]
        values = jnp.concatenate([values, jnp.ones((8, values.shape[1]), WIDE)]).astype(NARROW)
        for first in range(0, tiles, pair):
            here = slice(first * TILE, (first + pair) * TILE)
            scores = jnp.dot(keys, queries[:, here], preferred_element_type=WIDE)
            columns = []
            for tile in range(first, first + pair):
                lanes = slice((tile - first) * TILE, (tile - first + 1) * TILE)
                blocks = [
                    scores[other * TILE : (other + 1) * TILE, lanes]
                    + jnp.where(latents[other] == latents[tile], 0.0, -1e30)
                    for other in range(tiles)
                ]
                peak = functools.reduce(jnp.maximum, blocks)
                peak = jnp.max(peak, axis=0, keepdims=True)
                raised = [jnp.exp2((block - peak) * factor).astype(NARROW) for block in blocks]
                columns.append(jnp.concatenate(raised, axis=0))
            summed = jnp.dot(values, jnp.concatenate(columns, axis=1), preferred_element_type=WIDE)
            mixed[lower : lower + HEAD_DIM, here] = summed[:HEAD_DIM] / summed[HEAD_DIM : HEAD_DIM + 1]
    attended_ref[...] = mixed[...].T.astype(NARROW)


def place_pieces(parts, depth, pieces, expand, reduce):
    row = lax.axis_index("row")
    for (offset, which), piece in zip(parts, pieces):
        start = pl.multiple_of((row ^ offset) * depth, 16) if depth < D else 0
        here = pl.ds(start, depth)
        if "e" in which:
            expand[here, :] = piece[:depth, :]
        if "r" in which:
            reduce[here, :] = piece[-depth:, :]


def complete_kernel(parts, depth, expand_before, reduce_before, *refs):
    pieces, (expand, reduce) = refs[:-2], refs[-2:]
    expand[...] = expand_before[...]
    reduce[...] = reduce_before[...]
    place_pieces(parts, depth, pieces, expand, reduce)


def pair_kernel(first, second, *refs):
    out_ref = refs[-1]
    count = first.shape[0]
    out_ref[:count, :] = first[...]
    out_ref[count:, :] = second[...]


def order_kernel(*refs):
    refs[-1][...] = jnp.zeros(refs[-1].shape, WIDE)


def shared_kernel(parts_ref, head_ref, _, out_ref, mark_ref, head, head_sem):
    fetch = pltpu.make_async_copy(head_ref, head, head_sem)
    fetch.start()
    count = parts_ref.shape[1]
    out_ref[:count, :] = jnp.sum(parts_ref[...], axis=0)
    fetch.wait()
    out_ref[count:, :] = head[...].astype(WIDE)
    mark_ref[...] = jnp.zeros(mark_ref.shape, WIDE)


def mlp_kernel(
    offsets, latent_ref, att_own, att_across, att_beside, att_diagonal, tokens_ref, terms_ref, out_weight, expand, reduce, *refs
):
    outs, (mark_ref, attended, mid) = refs[-3 - len(offsets) - (0 in offsets) : -3], refs[-3:]
    mark_ref[...] = jnp.zeros(mark_ref.shape, WIDE)
    col = lax.axis_index("col")
    width = att_own.shape[1]
    tile_list = [col ^ offset for offset in offsets]
    starts = [pl.multiple_of(tile * TILE, TILE) for tile in tile_list]
    for place, block in enumerate((att_own, att_across, att_beside, att_diagonal)):
        for slot, start in enumerate(starts):
            here = slice(slot * TILE, (slot + 1) * TILE)
            attended[here, place * width : (place + 1) * width] = block[pl.ds(start, TILE), :]
    attn_sum = jnp.dot(attended[...], out_weight[...], preferred_element_type=WIDE)
    for slot, tile in enumerate(tile_list):
        term = functools.partial(tile_term, latent_ref, terms_ref, tile=tile)
        here = slice(slot * TILE, (slot + 1) * TILE)
        before = tokens_ref[pl.ds(starts[slot], TILE), :].astype(WIDE)
        residual = (before + term(2) * attn_sum[here]).astype(NARROW)
        if offsets[slot] == 0:
            outs[-1][...] = residual
        mid[here, :] = normalize(residual.astype(WIDE), term(3), term(4)).astype(NARROW)
    units = jnp.dot(mid[...], expand[...], preferred_element_type=WIDE)
    inner = 0.7978845608028654 * (units + 0.044715 * (units * units * units))
    activated = (0.5 * units * (1.0 + jnp.tanh(inner))).astype(NARROW)
    summed = lax.dot_general(activated, reduce[...], NT, preferred_element_type=WIDE)
    for slot, out in enumerate(outs[: len(offsets)]):
        out[...] = summed[slot * TILE : (slot + 1) * TILE].astype(out.dtype)


def head_kernel(latent_ref, kept_ref, beside_ref, crossed_ref, residual_ref, terms_ref, out_ref):
    col = lax.axis_index("col")
    term = functools.partial(tile_term, latent_ref, terms_ref, tile=col)
    mlp_sum = kept_ref[...] + beside_ref[...].astype(WIDE) + crossed_ref[...].astype(WIDE)
    second = (residual_ref[...].astype(WIDE) + term(5) * mlp_sum).astype(NARROW).astype(WIDE)
    normed = normalize(second, term(6), term(7)).astype(NARROW)
    group = PATCH * CHANNELS
    token_place = lax.broadcasted_iota(jnp.int32, (TILE, IMG_WIDTH), 0) % GRIDW
    lane_place = lax.broadcasted_iota(jnp.int32, (TILE, IMG_WIDTH), 1) // group
    for dy in range(PATCH):
        rows = terms_ref[16 + dy * group : 16 + (dy + 1) * group, :].astype(NARROW)
        spread_rows = jnp.concatenate([rows.astype(WIDE)] * GRIDW, axis=0).astype(NARROW)
        noise = lax.dot_general(normed, spread_rows, NT, preferred_element_type=WIDE)
        noise = jnp.where(token_place == lane_place, noise, 0.0)
        folded = jnp.sum(noise.reshape(TILE_ROWS, GRIDW, IMG_WIDTH), axis=1)
        out_ref[:, dy * IMG_WIDTH : (dy + 1) * IMG_WIDTH] = folded


def fill_bands(kernel_ref, out_ref):
    shape = (IMG_WIDTH, IMG_WIDTH)
    source = lax.broadcasted_iota(jnp.int32, shape, 0)
    target = lax.broadcasted_iota(jnp.int32, shape, 1)
    reach = 3 * CHANNELS
    apart = target - (source // CHANNELS) * CHANNELS + CHANNELS
    code = jnp.where((apart >= 0) & (apart < reach), (source % CHANNELS) * reach + apart, -1)
    bands = [jnp.zeros(shape, WIDE) for _ in range(3)]
    for channel in range(CHANNELS):
        for lane in range(reach):
            here = code == channel * reach + lane
            column, out_channel = 2 - lane // CHANNELS, lane % CHANNELS
            for line in range(3):
                value = kernel_ref[line, column, channel, out_channel]
                bands[line] = jnp.where(here, value, bands[line])
    for line in range(3):
        out_ref[:, line * IMG_WIDTH : (line + 1) * IMG_WIDTH] = bands[line]


def step_kernel(
    table_ref, now_ref, next_ref, near, far, noisy_ref, bands_ref,
    stepped_ref, preview_ref, image, clean, above, below,
):
    tiles = noisy_ref.shape[0] // IMG_ROWS
    row = lax.axis_index("row")
    tile_count = lax.axis_size("row") * tiles
    col = lax.axis_index("col")
    for place in range(4):

        @pl.when(col == place)
        def _():
            for offset in range(4):
                block = (near, far)[offset // 2]
                rows = slice(offset % 2 * TILE_ROWS, (offset % 2 + 1) * TILE_ROWS)
                for dy in range(PATCH):
                    start = (place ^ offset) * IMG_ROWS + dy
                    image[pl.ds(start, TILE_ROWS, PATCH), :] = block[rows, dy * IMG_WIDTH : (dy + 1) * IMG_WIDTH]

    for tile in range(tiles):
        here = slice(tile * IMG_ROWS, (tile + 1) * IMG_ROWS)
        step = table_ref[tile_count + table_ref[row * tiles + tile]]
        signal_now = jnp.full((1, IMG_WIDTH), now_ref[step], WIDE)
        signal_next = jnp.full((1, IMG_WIDTH), next_ref[step], WIDE)
        noise = image[here, :]
        rows = (noisy_ref[here, :].astype(WIDE) - jnp.sqrt(1.0 - signal_now) * noise) / jnp.sqrt(signal_now)
        clean[here, :] = rows
        stepped = jnp.sqrt(signal_next) * rows + jnp.sqrt(1.0 - signal_next) * noise
        stepped_ref[here, :] = stepped.astype(NARROW)
    parts = jnp.dot(
        clean[...], bands_ref[...], precision=lax.Precision.HIGHEST, preferred_element_type=WIDE
    )
    count = tiles * IMG_ROWS
    above[8 : 8 + count, :] = parts[:, :IMG_WIDTH]
    below[8 : 8 + count, :] = parts[:, 2 * IMG_WIDTH :]
    for tile in range(tiles):
        here = slice(tile * IMG_ROWS, (tile + 1) * IMG_ROWS)
        start = 8 + tile * IMG_ROWS
        line = lax.broadcasted_iota(jnp.int32, (IMG_ROWS, IMG_WIDTH), 0)
        from_above = above[start - 1 : start - 1 + IMG_ROWS, :]
        from_below = below[start + 1 : start + 1 + IMG_ROWS, :]
        mine = table_ref[row * tiles + tile]
        if tile == 0:
            above_ok = line > 0
        else:
            above_ok = (line > 0) | (table_ref[row * tiles + tile - 1] == mine)
        if tile == tiles - 1:
            below_ok = line < IMG_ROWS - 1
        else:
            below_ok = (line < IMG_ROWS - 1) | (table_ref[row * tiles + tile + 1] == mine)
        total = parts[here, IMG_WIDTH : 2 * IMG_WIDTH]
        total = total + jnp.where(above_ok, from_above, 0.0) + jnp.where(below_ok, from_below, 0.0)
        preview_ref[here, :] = total.astype(NARROW)


def shards(
    hidden,
    noisy_latent,
    tile_latent,
    timesteps,
    step_embedding,
    alpha_now,
    alpha_next,
    modulation,
    attention_in,
    attention_out,
    expand_weight,
    reduce_weight,
    noise_head,
    preview_kernel,
):
    rows = lax.axis_size("row")
    tokens_here, width = hidden.shape
    tiles = tokens_here // TILE
    depth = modulation.shape[0]
    units = expand_weight.shape[1]
    shape = jax.ShapeDtypeStruct

    table = jnp.concatenate([tile_latent, timesteps])
    mark = shape((8, 128), WIDE)
    conditioning, conditioned = call(
        functools.partial(condition_kernel, tiles),
        [shape((2 * rows, depth), NARROW), mark],
        [SMEM, VMEM],
        [pltpu.VMEM((2 * rows, STEPS), WIDE)],
        flops=2 * 2 * rows * D * (STEPS + depth), nbytes=2 * STEPS * D,
    )(table, step_embedding)
    partial = jnp.einsum("td,dkc->tkc", conditioning, modulation, preferred_element_type=WIDE)
    partial = partial.reshape(rows, 16, width)
    received = lax.all_to_all(partial, "row", 0, 0, tiled=True)
    blocks_here = jnp.concatenate([hidden.T, attention_out], axis=1)
    blocks_across = exchange(blocks_here, "col", 2)
    reduce_rows = reduce_weight.T
    staged = rows == 8
    if staged:
        both = jnp.concatenate([expand_weight, reduce_rows], axis=0)
        both_4 = exchange(both, "row", 4)
        both_2 = exchange(both, "row", 2)
        both_1 = exchange(both, "row", 1)
        first, middle = [], []
        if F.get("f4", 0) < 2:
            (first, middle)[F.get("f4", 0)].append(both_4)
        (first if F.get("f2", 1) else middle).append(both_2)
        (first if F.get("f1", 1) else middle).append(both_1)
    else:
        expand_whole = lax.all_gather(expand_weight, "row", axis=0, tiled=True)
        reduce_whole = lax.all_gather(reduce_rows, "row", axis=0, tiled=True)
        first, middle = [], []
    arrived = call(order_kernel, mark, [ANYWHERE] * (1 + len(first)))(conditioned, *first)
    shared, shared_done = call(
        shared_kernel, [shape((32, width), WIDE), mark], [VMEM] + [ANYWHERE] * 2,
        [pltpu.VMEM((16, width), NARROW), pltpu.SemaphoreType.DMA], nbytes=2**18,
    )(received, noise_head.T, arrived)
    terms_near = pack(shared, exchange(shared, "col", 1), *middle)
    terms_far = exchange(terms_near, "col", 2)
    near = pack(blocks_here, blocks_across, *([terms_near] if F.get("np", 1) else [shared_done]))
    far = exchange(near, "col", 1)
    second, third = [], []
    if staged:
        both_3 = exchange(both_2, "row", 1)
        both_6 = exchange(both_4, "row", 2)
        both_5 = exchange(both_4, "row", 1)
        both_7 = exchange(both_6, "row", 1)
        second, third = [], []
        if F.get("f4", 0) > 1:
            (second, third)[F["f4"] - 2].append(both_4)
        for name, piece in (("p3", both_3), ("p6", both_6), ("p5", both_5)):
            place = F.get(name, 1 if name != "p5" else 2)
            if place:
                (second, third)[place - 1].append(piece)
        parts = [(i, "er", piece) for i, piece in enumerate((both, both_1, both_2, both_3, both_4, both_5, both_6))]
        last = [(7, "er", both_7)]
    else:
        parts, last = [(0, "e", expand_whole), (0, "r", reduce_whole)], []
    attention_weight = attention_in.transpose(1, 2, 0).reshape(3 * width, D)
    terms, columns = call(
        terms_kernel, [shape((32, D), WIDE), shape((D, 32), WIDE)], [VMEM] * 2, flops=F.get("tc", 4) * 10**9
    )(terms_near, terms_far)
    triple = call(
        triple_kernel,
        shape((3 * width, tokens_here), WIDE),
        [SMEM] + [VMEM] * 3 + [ANYWHERE] * (1 + len(second)),
        [
            pltpu.VMEM((3 * width, D), NARROW),
            pltpu.SemaphoreType.DMA,
            pltpu.VMEM((D, tokens_here), NARROW),
        ],
        flops=2 * tokens_here * D * 3 * width, nbytes=5 * 2**20, limit=16,
    )(table, near, far, columns, attention_weight, *second)
    attended, attention_done = call(
        attention_kernel,
        [shape((tokens_here, width), NARROW), mark],
        [SMEM, VMEM] + [ANYWHERE] * len(third),
        [pltpu.VMEM((width, tokens_here), WIDE)],
        flops=4 * tokens_here * tokens_here * width, trans=4 * tokens_here**2, limit=16,
    )(table, triple, *third)
    split = depth if staged else D
    out_weight, expand_all, reduce_all, tokens, bands = call(
        functools.partial(assemble_kernel, [part[:2] for part in parts], split),
        [
            shape((D, D), NARROW),
            shape((D, units), NARROW),
            shape((D, units), NARROW),
            shape((tokens_here, D), NARROW),
            shape((IMG_WIDTH, 3 * IMG_WIDTH), WIDE),
        ],
        [SMEM] + [VMEM] * (2 + len(parts)) + [ANYWHERE],
        nbytes=2**23, limit=24,
    )(preview_kernel, near, far, *(part[2] for part in parts), attention_done)
    across = exchange(attended, "col", 2)
    if F.get("pass", 0) == 0:
        passed = call(pass_kernel, shape(across.shape, NARROW), [VMEM, ANYWHERE], nbytes=2**19)(across, tokens)
    else:
        passed = across
    attended_blocks = (attended, across, exchange(attended, "col", 1), exchange(passed, "col", 1))
    if last:
        expand_all, reduce_all = call(
            functools.partial(complete_kernel, [part[:2] for part in last], split),
            [shape((D, units), NARROW)] * 2, [VMEM] * (2 + len(last)), nbytes=2**22, limit=8,
        )(expand_all, reduce_all, *(part[2] for part in last))

    def mlp(offsets, *before):
        outs = [shape((TILE, D), NARROW if offset % 2 else WIDE) for offset in offsets]
        if 0 in offsets:
            outs.append(shape((TILE, D), NARROW))
        outs.append(mark)
        count = len(offsets) * TILE
        return call(
            functools.partial(mlp_kernel, offsets),
            outs,
            [SMEM] + [VMEM] * 9 + [ANYWHERE] * len(before),
            [pltpu.VMEM((count, D), NARROW)] * 2,
            flops=2 * count * D * (D + 2 * units), nbytes=8 * 2**20, trans=count * units, limit=20,
        )(table, *attended_blocks, tokens, terms, out_weight, expand_all, reduce_all, *before)

    far_kept, far_sent, far_done = mlp((2, 3))
    tail = F.get("tail", 0)
    if tail == 0:
        near_sent, _ = mlp((1,), far_done)
    far_sum = (far_kept + exchange(far_sent, "col", 1).astype(WIDE)).astype(NARROW)
    crossed = exchange(far_sum, "col", 2)
    if tail == 1:
        near_sent, _ = mlp((1,), far_sum)
    if tail < 2:
        near_kept, residual, _ = mlp((0,), far_sum)
    else:
        near_kept, near_sent, residual, _ = mlp((0, 1), far_sum)
    beside = exchange(near_sent, "col", 1)
    noise = call(
        head_kernel,
        shape((TILE_ROWS, PATCH * IMG_WIDTH), WIDE),
        [SMEM] + [VMEM] * 5,
        flops=4 * TILE * D * IMG_WIDTH, nbytes=2**21, limit=8,
    )(table, near_kept, beside, crossed, residual, terms)

    noise_near = pack(noise, exchange(noise, "col", 1))
    img_rows = tiles * IMG_ROWS
    stepped, preview = call(
        step_kernel,
        [shape((img_rows, IMG_WIDTH), NARROW)] * 2,
        [SMEM] * 3 + [VMEM] * 4,
        [pltpu.VMEM((img_rows, IMG_WIDTH), WIDE)] * 2
        + [pltpu.VMEM((img_rows + 16, IMG_WIDTH), WIDE)] * 2,
        flops=12 * img_rows * IMG_WIDTH**2, nbytes=2**19,
    )(table, alpha_now, alpha_next, noise_near, exchange(noise_near, "col", 2), noisy_latent, bands)
    return (stepped, preview)


def solution(mesh):
    return jax.shard_map(
        shards,
        mesh=mesh,
        in_specs=(
            P("row", "col"),
            P("row", None),
            P(),
            P(),
            P(),
            P(),
            P(),
            P("row", None, "col"),
            P(None, None, "col"),
            P("col", None),
            P("row", "col"),
            P("col", "row"),
            P("col", None),
            P(),
        ),
        out_specs=(P("row", None), P("row", None)),
        check_vma=False,
    )
```

```python
import functools

import jax
import jax.numpy as jnp
from jax import lax
from jax.experimental import pallas as pl
from jax.experimental.pallas import tpu as pltpu
from jax.sharding import PartitionSpec as P

D = 1152
HEAD_DIM = 72
PATCH = 2
CHANNELS = 4
GRIDW = 16
NOISE = PATCH * PATCH * CHANNELS
F = {'p3': 0, 'p6': 0, 'p5': 0, 'at': ['both_6'], 'l3': 0}
COSTS = {}
COUNT = [0]
TILE_ROWS = 8
STEPS = 50
TILE = 128
EPS_NORM = 1e-06
IMG_ROWS = TILE_ROWS * PATCH
IMG_WIDTH = GRIDW * PATCH * CHANNELS
WIDE = jnp.float32
NARROW = jnp.bfloat16
NT = (((1,), (1,)), ((), ()))
VMEM = pl.BlockSpec(memory_space=pltpu.VMEM)
SMEM = pl.BlockSpec(memory_space=pltpu.SMEM)
ANYWHERE = pl.BlockSpec(memory_space=pl.ANY)
MIB = 1024 * 1024


def call(kernel, outs, in_specs, scratch=(), flops=0, nbytes=0, trans=0, limit=4):
    base = getattr(kernel, "func", kernel).__name__
    COUNT[0] += 1
    if base in COSTS:
        flops, nbytes, trans = int(COSTS[base] * 10**9), 0, 0
    return pl.pallas_call(
        kernel,
        out_shape=outs,
        in_specs=in_specs,
        out_specs=jax.tree.map(lambda _: VMEM, outs),
        scratch_shapes=list(scratch),
        compiler_params=pltpu.CompilerParams(vmem_limit_bytes=limit * MIB),
        cost_estimate=pl.CostEstimate(flops=flops, bytes_accessed=nbytes, transcendentals=trans),
    )


def exchange(value, axis, offset):
    size = lax.axis_size(axis)
    return lax.ppermute(value, axis, [(i, i ^ offset) for i in range(size)])


def gather_blocks(value):
    across = exchange(value, "col", 2)
    beside = exchange(value, "col", 1)
    diagonal = exchange(across, "col", 1)
    return value, beside, across, diagonal


def after_kernel(*_):
    pass


def after(value, *before):
    return pl.pallas_call(
        after_kernel,
        out_shape=jax.ShapeDtypeStruct(value.shape, value.dtype),
        in_specs=[ANYWHERE] * (1 + len(before)),
        out_specs=ANYWHERE,
        input_output_aliases={0: 0},
        compiler_params=pltpu.CompilerParams(vmem_limit_bytes=MIB),
        cost_estimate=pl.CostEstimate(flops=0, bytes_accessed=0, transcendentals=0),
    )(value, *before)


def pack(first, second, *before):
    out = jax.ShapeDtypeStruct((2 * first.shape[0], first.shape[1]), first.dtype)
    return call(pair_kernel, out, [VMEM] * 2 + [ANYWHERE] * len(before), limit=8)(first, second, *before)


def normalize(values, shift_term, scale_term):
    mean_value = jnp.sum(values, axis=-1, keepdims=True) * (1.0 / D)
    spread = jnp.sum(values * values, axis=-1, keepdims=True) * (1.0 / D) - mean_value * mean_value
    normed = (values - mean_value) * lax.rsqrt(spread + EPS_NORM)
    return normed * (1.0 + scale_term) + shift_term


def condition_kernel(tiles_here, table_ref, embedding_ref, out_ref, mark_ref, onehot):
    count, depth = out_ref.shape
    tile_count = count // 2 * tiles_here
    mark_ref[...] = jnp.zeros(mark_ref.shape, WIDE)

    def pick(index, carry):
        tile = (index // 2) * tiles_here + (index % 2) * (tiles_here - 1)
        step = table_ref[tile_count + table_ref[tile]]
        lanes = lax.broadcasted_iota(jnp.int32, (1, STEPS), 1)
        onehot[pl.ds(index, 1), :] = jnp.where(lanes == step, 1.0, 0.0)
        return carry

    lax.fori_loop(0, count, pick, 0)
    embedded = jnp.dot(onehot[...].astype(NARROW), embedding_ref[...], preferred_element_type=WIDE)
    conditioning = (embedded / (1.0 + jnp.exp(-embedded))).astype(NARROW)
    first = lax.axis_index("row") * depth
    source = lax.broadcasted_iota(jnp.int32, (D, depth), 0)
    target = lax.broadcasted_iota(jnp.int32, (D, depth), 1) + first
    chosen = jnp.where(source == target, 1.0, 0.0).astype(NARROW)
    out_ref[...] = jnp.dot(conditioning, chosen, preferred_element_type=WIDE).astype(NARROW)


def tile_term(latent_ref, terms_ref, index, tile):
    first = lax.axis_index("row") * (lax.axis_size("col"))
    later = latent_ref[first + tile] != latent_ref[first]
    return jnp.where(later, terms_ref[8 + index : 9 + index, :], terms_ref[index : index + 1, :])


def pass_kernel(*refs):
    refs[-1][...] = refs[0][...]


def terms_kernel(terms_near, terms_far, *refs):
    col = lax.axis_index("col")
    width = terms_near.shape[1]
    terms_ref, columns = refs[-2:]
    rows = terms_ref.shape[0]
    for place in range(4):

        @pl.when(col == place)
        def _():
            for offset in range(4):
                block = (terms_near, terms_far)[offset // 2]
                lower = (place ^ offset) * width
                terms_ref[:, lower : lower + width] = block[offset % 2 * rows : (offset % 2 + 1) * rows, :]

    columns[...] = terms_ref[...].T


def triple_kernel(latent_ref, own, beside, across, diagonal, columns, weight_ref, *refs):
    triple_ref, weight, weight_sem, normed = refs[-4:]
    fetch = pltpu.make_async_copy(weight_ref, weight, weight_sem)
    fetch.start()
    col = lax.axis_index("col")
    width, count = own.shape[0], triple_ref.shape[1]
    blocks = [source[:, :count] for source in (own, beside, across, diagonal)]
    total = jnp.zeros((1, count), WIDE)
    squares = jnp.zeros((1, count), WIDE)
    for block in blocks:
        values = block.astype(WIDE)
        total = total + jnp.sum(values, axis=0, keepdims=True)
        squares = squares + jnp.sum(values * values, axis=0, keepdims=True)
    mean_value = total * (1.0 / D)
    spread = squares * (1.0 / D) - mean_value * mean_value
    rate = lax.rsqrt(spread + EPS_NORM)
    first = lax.axis_index("row") * (count // TILE)
    later = [latent_ref[first + tile] != latent_ref[first] for tile in range(count // TILE)]
    for offset, block in enumerate(blocks):
        here = pl.ds(pl.multiple_of((col ^ offset) * width, 32), width)
        shifts = [jnp.broadcast_to(columns[here, at : at + 1], (width, TILE)) for at in (0, 8)]
        scales = [jnp.broadcast_to(columns[here, at : at + 1], (width, TILE)) + 1.0 for at in (1, 9)]
        for tile in range(count // TILE):
            lanes = slice(tile * TILE, (tile + 1) * TILE)
            values = (block[:, lanes].astype(WIDE) - mean_value[:, lanes]) * rate[:, lanes]
            scale = jnp.where(later[tile], scales[1], scales[0])
            shift = jnp.where(later[tile], shifts[1], shifts[0])
            normed[here, lanes] = (values * scale + shift).astype(NARROW)
    fetch.wait()
    triple_ref[...] = jnp.dot(weight[...], normed[...], preferred_element_type=WIDE)


def assemble_kernel(parts, depth, kernel_ref, own, beside, across, diagonal, *refs):
    pieces, (out_weight, expand, reduce, tokens_ref, head_ref, bands_ref) = refs[: len(parts)], refs[-6:]
    col = lax.axis_index("col")
    width, count = own.shape[0], tokens_ref.shape[0]
    for index, source in enumerate((own, across, beside, diagonal)):
        out_weight[index * width : (index + 1) * width, :] = source[:, count : count + D]
    for offset, source in enumerate((own, beside, across, diagonal)):
        head_ref[pl.ds(pl.multiple_of((col ^ offset) * width, 16), width), :] = source[:, count + D :]
    place_pieces(parts, depth, pieces, expand, reduce)
    for place in range(4):

        @pl.when(col == place)
        def _():
            for offset, source in enumerate((own, beside, across, diagonal)):
                lower = (place ^ offset) * width
                tokens_ref[:, lower : lower + width] = source[:, :count].T

    fill_bands(kernel_ref, bands_ref)


def attention_kernel(latent_ref, triple, *refs):
    attended_ref, mark_ref, mixed = refs[-3:]
    mark_ref[...] = jnp.zeros(mark_ref.shape, WIDE)
    row = lax.axis_index("row")
    width = attended_ref.shape[1]
    tiles = attended_ref.shape[0] // TILE
    latents = [latent_ref[row * tiles + tile] for tile in range(tiles)]
    factor = HEAD_DIM ** (-0.5) * 1.4426950408889634
    pair = 2
    for head in range(width // HEAD_DIM):
        lower = head * HEAD_DIM
        queries = triple[lower : lower + HEAD_DIM, :].astype(NARROW)
        keys = triple[width + lower : width + lower + HEAD_DIM, :].T.astype(NARROW)
        values = triple[2 * width + lower : 2 * width + lower + HEAD_DIM, :]
        values = jnp.concatenate([values, jnp.ones((8, values.shape[1]), WIDE)]).astype(NARROW)
        for first in range(0, tiles, pair):
            here = slice(first * TILE, (first + pair) * TILE)
            scores = jnp.dot(keys, queries[:, here], preferred_element_type=WIDE)
            columns = []
            for tile in range(first, first + pair):
                lanes = slice((tile - first) * TILE, (tile - first + 1) * TILE)
                blocks = [
                    scores[other * TILE : (other + 1) * TILE, lanes]
                    + jnp.where(latents[other] == latents[tile], 0.0, -1e30)
                    for other in range(tiles)
                ]
                peak = functools.reduce(jnp.maximum, blocks)
                peak = jnp.max(peak, axis=0, keepdims=True)
                raised = [jnp.exp2((block - peak) * factor).astype(NARROW) for block in blocks]
                columns.append(jnp.concatenate(raised, axis=0))
            summed = jnp.dot(values, jnp.concatenate(columns, axis=1), preferred_element_type=WIDE)
            mixed[lower : lower + HEAD_DIM, here] = summed[:HEAD_DIM] / summed[HEAD_DIM : HEAD_DIM + 1]
    attended_ref[...] = mixed[...].T.astype(NARROW)


def place_pieces(parts, depth, pieces, expand, reduce):
    row = lax.axis_index("row")
    for (offset, which), piece in zip(parts, pieces):
        start = pl.multiple_of((row ^ offset) * depth, 16) if depth < D else 0
        here = pl.ds(start, depth)
        if "e" in which:
            expand[here, :] = piece[:depth, :]
        if "r" in which:
            reduce[here, :] = piece[-depth:, :]


def complete_kernel(parts, depth, expand_before, reduce_before, *refs):
    pieces, (expand, reduce) = refs[:-2], refs[-2:]
    expand[...] = expand_before[...]
    reduce[...] = reduce_before[...]
    place_pieces(parts, depth, pieces, expand, reduce)


def pair_kernel(first, second, *refs):
    out_ref = refs[-1]
    count = first.shape[0]
    out_ref[:count, :] = first[...]
    out_ref[count:, :] = second[...]


def order_kernel(*refs):
    refs[-1][...] = jnp.zeros(refs[-1].shape, WIDE)


def shared_kernel(parts_ref, _, out_ref):
    out_ref[...] = jnp.sum(parts_ref[...], axis=0)


def mlp_kernel(
    offsets, latent_ref, att_own, att_across, att_beside, att_diagonal, tokens_ref, terms_ref, out_weight, expand, reduce, *refs
):
    outs, (mark_ref, attended, mid) = refs[-3 - len(offsets) - (0 in offsets) : -3], refs[-3:]
    mark_ref[...] = jnp.zeros(mark_ref.shape, WIDE)
    col = lax.axis_index("col")
    width = att_own.shape[1]
    tile_list = [col ^ offset for offset in offsets]
    starts = [pl.multiple_of(tile * TILE, TILE) for tile in tile_list]
    for place, block in enumerate((att_own, att_across, att_beside, att_diagonal)):
        for slot, start in enumerate(starts):
            here = slice(slot * TILE, (slot + 1) * TILE)
            attended[here, place * width : (place + 1) * width] = block[pl.ds(start, TILE), :]
    attn_sum = jnp.dot(attended[...], out_weight[...], preferred_element_type=WIDE)
    for slot, tile in enumerate(tile_list):
        term = functools.partial(tile_term, latent_ref, terms_ref, tile=tile)
        here = slice(slot * TILE, (slot + 1) * TILE)
        before = tokens_ref[pl.ds(starts[slot], TILE), :].astype(WIDE)
        residual = (before + term(2) * attn_sum[here]).astype(NARROW)
        if offsets[slot] == 0:
            outs[-1][...] = residual
        mid[here, :] = normalize(residual.astype(WIDE), term(3), term(4)).astype(NARROW)
    units = jnp.dot(mid[...], expand[...], preferred_element_type=WIDE)
    inner = 0.7978845608028654 * (units + 0.044715 * (units * units * units))
    activated = (0.5 * units * (1.0 + jnp.tanh(inner))).astype(NARROW)
    summed = lax.dot_general(activated, reduce[...], NT, preferred_element_type=WIDE)
    for slot, out in enumerate(outs[: len(offsets)]):
        out[...] = summed[slot * TILE : (slot + 1) * TILE].astype(out.dtype)


def head_kernel(latent_ref, kept_ref, beside_ref, crossed_ref, residual_ref, terms_ref, head_ref, out_ref):
    col = lax.axis_index("col")
    term = functools.partial(tile_term, latent_ref, terms_ref, tile=col)
    mlp_sum = kept_ref[...] + beside_ref[...].astype(WIDE) + crossed_ref[...].astype(WIDE)
    second = (residual_ref[...].astype(WIDE) + term(5) * mlp_sum).astype(NARROW).astype(WIDE)
    normed = normalize(second, term(6), term(7)).astype(NARROW)
    group = PATCH * CHANNELS
    token_place = lax.broadcasted_iota(jnp.int32, (TILE, IMG_WIDTH), 0) % GRIDW
    lane_place = lax.broadcasted_iota(jnp.int32, (TILE, IMG_WIDTH), 1) // group
    source = lax.broadcasted_iota(jnp.int32, (NOISE, PATCH * IMG_WIDTH), 0)
    target = lax.broadcasted_iota(jnp.int32, (NOISE, PATCH * IMG_WIDTH), 1)
    chosen = jnp.where(source == target // IMG_WIDTH * group + target % group, 1.0, 0.0).astype(NARROW)
    spread_head = jnp.dot(head_ref[...], chosen, preferred_element_type=WIDE).astype(NARROW)
    noise = jnp.dot(normed, spread_head, preferred_element_type=WIDE)
    for dy in range(PATCH):
        lanes = slice(dy * IMG_WIDTH, (dy + 1) * IMG_WIDTH)
        kept = jnp.where(token_place == lane_place, noise[:, lanes], 0.0)
        out_ref[:, lanes] = jnp.sum(kept.reshape(TILE_ROWS, GRIDW, IMG_WIDTH), axis=1)


def fill_bands(kernel_ref, out_ref):
    shape = (IMG_WIDTH, IMG_WIDTH)
    source = lax.broadcasted_iota(jnp.int32, shape, 0)
    target = lax.broadcasted_iota(jnp.int32, shape, 1)
    reach = 3 * CHANNELS
    apart = target - (source // CHANNELS) * CHANNELS + CHANNELS
    code = jnp.where((apart >= 0) & (apart < reach), (source % CHANNELS) * reach + apart, -1)
    bands = [jnp.zeros(shape, WIDE) for _ in range(3)]
    for channel in range(CHANNELS):
        for lane in range(reach):
            here = code == channel * reach + lane
            column, out_channel = 2 - lane // CHANNELS, lane % CHANNELS
            for line in range(3):
                value = kernel_ref[line, column, channel, out_channel]
                bands[line] = jnp.where(here, value, bands[line])
    for line in range(3):
        out_ref[:, line * IMG_WIDTH : (line + 1) * IMG_WIDTH] = bands[line]


def step_kernel(
    table_ref, now_ref, next_ref, near, far, noisy_ref, bands_ref,
    stepped_ref, preview_ref, image, clean, above, below,
):
    tiles = noisy_ref.shape[0] // IMG_ROWS
    row = lax.axis_index("row")
    tile_count = lax.axis_size("row") * tiles
    col = lax.axis_index("col")
    for place in range(4):

        @pl.when(col == place)
        def _():
            for offset in range(4):
                block = (near, far)[offset // 2]
                rows = slice(offset % 2 * TILE_ROWS, (offset % 2 + 1) * TILE_ROWS)
                for dy in range(PATCH):
                    start = (place ^ offset) * IMG_ROWS + dy
                    image[pl.ds(start, TILE_ROWS, PATCH), :] = block[rows, dy * IMG_WIDTH : (dy + 1) * IMG_WIDTH]

    for tile in range(tiles):
        here = slice(tile * IMG_ROWS, (tile + 1) * IMG_ROWS)
        step = table_ref[tile_count + table_ref[row * tiles + tile]]
        signal_now = jnp.full((1, IMG_WIDTH), now_ref[step], WIDE)
        signal_next = jnp.full((1, IMG_WIDTH), next_ref[step], WIDE)
        noise = image[here, :]
        rows = (noisy_ref[here, :].astype(WIDE) - jnp.sqrt(1.0 - signal_now) * noise) / jnp.sqrt(signal_now)
        clean[here, :] = rows
        stepped = jnp.sqrt(signal_next) * rows + jnp.sqrt(1.0 - signal_next) * noise
        stepped_ref[here, :] = stepped.astype(NARROW)
    parts = jnp.dot(
        clean[...], bands_ref[...], precision=lax.Precision.HIGHEST, preferred_element_type=WIDE
    )
    count = tiles * IMG_ROWS
    above[8 : 8 + count, :] = parts[:, :IMG_WIDTH]
    below[8 : 8 + count, :] = parts[:, 2 * IMG_WIDTH :]
    for tile in range(tiles):
        here = slice(tile * IMG_ROWS, (tile + 1) * IMG_ROWS)
        start = 8 + tile * IMG_ROWS
        line = lax.broadcasted_iota(jnp.int32, (IMG_ROWS, IMG_WIDTH), 0)
        from_above = above[start - 1 : start - 1 + IMG_ROWS, :]
        from_below = below[start + 1 : start + 1 + IMG_ROWS, :]
        mine = table_ref[row * tiles + tile]
        if tile == 0:
            above_ok = line > 0
        else:
            above_ok = (line > 0) | (table_ref[row * tiles + tile - 1] == mine)
        if tile == tiles - 1:
            below_ok = line < IMG_ROWS - 1
        else:
            below_ok = (line < IMG_ROWS - 1) | (table_ref[row * tiles + tile + 1] == mine)
        total = parts[here, IMG_WIDTH : 2 * IMG_WIDTH]
        total = total + jnp.where(above_ok, from_above, 0.0) + jnp.where(below_ok, from_below, 0.0)
        preview_ref[here, :] = total.astype(NARROW)


def shards(
    hidden,
    noisy_latent,
    tile_latent,
    timesteps,
    step_embedding,
    alpha_now,
    alpha_next,
    modulation,
    attention_in,
    attention_out,
    expand_weight,
    reduce_weight,
    noise_head,
    preview_kernel,
):
    rows = lax.axis_size("row")
    tokens_here, width = hidden.shape
    tiles = tokens_here // TILE
    depth = modulation.shape[0]
    units = expand_weight.shape[1]
    shape = jax.ShapeDtypeStruct

    table = jnp.concatenate([tile_latent, timesteps])
    mark = shape((8, 128), WIDE)
    conditioning, conditioned = call(
        functools.partial(condition_kernel, tiles),
        [shape((2 * rows, depth), NARROW), mark],
        [SMEM, VMEM],
        [pltpu.VMEM((2 * rows, STEPS), WIDE)],
        flops=2 * 2 * rows * D * (STEPS + depth), nbytes=2 * STEPS * D,
    )(table, step_embedding)
    partial = jnp.einsum("td,dkc->tkc", conditioning, modulation, preferred_element_type=WIDE)
    partial = partial.reshape(rows, 16, width)
    received = lax.all_to_all(partial, "row", 0, 0, tiled=True)
    blocks_here = jnp.concatenate([hidden.T, attention_out, noise_head], axis=1)
    blocks_across = exchange(blocks_here, "col", 2)
    reduce_rows = reduce_weight.T
    staged = rows == 8
    if staged:
        both = jnp.concatenate([expand_weight, reduce_rows], axis=0)
        both_4 = exchange(both, "row", 4)
        both_2 = exchange(both, "row", 2)
        both_1 = exchange(both, "row", 1)
        first, middle = [], []
        if F.get("f4", 0) < 2:
            (first, middle)[F.get("f4", 0)].append(both_4)
        (first if F.get("f2", 1) else middle).append(both_2)
        (first if F.get("f1", 1) else middle).append(both_1)
    else:
        expand_whole = lax.all_gather(expand_weight, "row", axis=0, tiled=True)
        reduce_whole = lax.all_gather(reduce_rows, "row", axis=0, tiled=True)
        first, middle = [], []
    arrived = call(order_kernel, mark, [ANYWHERE] * (1 + len(first)))(conditioned, *first)
    shared = call(shared_kernel, shape((16, width), WIDE), [VMEM, ANYWHERE], nbytes=2**18)(received, arrived)
    at_near, at_terms = [], []
    second, third = [], []
    if staged:
        both_3 = exchange(both_2, "row", 1)
        both_6 = exchange(both_4, "row", 2)
        both_5 = exchange(both_4, "row", 1)
        both_7 = exchange(both_5, "row", 2) if F.get("w5", 1) else exchange(both_6, "row", 1)
        second, third = [], []
        if F.get("f4", 0) > 1:
            (second, third)[F["f4"] - 2].append(both_4)
        for name, piece in (("p3", both_3), ("p6", both_6), ("p5", both_5)):
            place = F.get(name, 1 if name != "p5" else 2)
            if place:
                (second, third, at_terms, at_near, middle)[place - 1].append(piece)
        parts = [(0, "er", both), (1, "er", both_1), (2, "er", both_2), (4, "er", both_4), (5, "er", both_5), (6, "er", both_6)]
        last = [(3, "er", both_3), (7, "er", both_7)]
        if not F.get("l3", 1):
            parts.append(last.pop(0))
    else:
        parts, last = [(0, "e", expand_whole), (0, "r", reduce_whole)], []
    terms_near = pack(shared, exchange(shared, "col", 1), *middle)
    terms_far = exchange(terms_near, "col", 2)
    blocks_across = after(blocks_across, terms_near)
    blocks = (blocks_here, exchange(blocks_here, "col", 1), blocks_across, exchange(blocks_across, "col", 1))
    attention_weight = attention_in.transpose(1, 2, 0).reshape(3 * width, D)
    terms, columns = call(
        terms_kernel, [shape((16, D), WIDE), shape((D, 16), WIDE)], [VMEM] * 2 + [ANYWHERE] * len(at_terms), flops=F.get("tc", 4) * 10**9
    )(terms_near, terms_far, *at_terms)
    triple = call(
        triple_kernel,
        shape((3 * width, tokens_here), WIDE),
        [SMEM] + [VMEM] * 5 + [ANYWHERE] * (1 + len(second)),
        [
            pltpu.VMEM((3 * width, D), NARROW),
            pltpu.SemaphoreType.DMA,
            pltpu.VMEM((D, tokens_here), NARROW),
        ],
        flops=2 * tokens_here * D * 3 * width, nbytes=5 * 2**20, limit=16,
    )(table, *blocks, columns, attention_weight, *second)
    attended, attention_done = call(
        attention_kernel,
        [shape((tokens_here, width), NARROW), mark],
        [SMEM, VMEM] + [ANYWHERE] * len(third),
        [pltpu.VMEM((width, tokens_here), WIDE)],
        flops=4 * tokens_here * tokens_here * width, trans=4 * tokens_here**2, limit=16,
    )(table, triple, *third)
    split = depth if staged else D
    out_weight, expand_all, reduce_all, tokens, head, bands = call(
        functools.partial(assemble_kernel, [part[:2] for part in parts], split),
        [
            shape((D, D), NARROW),
            shape((D, units), NARROW),
            shape((D, units), NARROW),
            shape((tokens_here, D), NARROW),
            shape((D, NOISE), NARROW),
            shape((IMG_WIDTH, 3 * IMG_WIDTH), WIDE),
        ],
        [SMEM] + [VMEM] * (4 + len(parts)) + [ANYWHERE],
        nbytes=2**23, limit=24,
    )(preview_kernel, *blocks, *(part[2] for part in parts), attention_done)
    ahead = [locals()[name] for name in F.get("at", ()) if staged]
    if ahead:
        attended = after(attended, *ahead)
    across = exchange(attended, "col", 2)
    if F.get("pass", 0) == 0:
        if F.get("pa", 0):
            passed = after(across, tokens)
            across = passed
        else:
            passed = call(pass_kernel, shape(across.shape, NARROW), [VMEM, ANYWHERE], nbytes=2**19)(across, tokens)
    else:
        passed = across
    attended_blocks = (attended, across, exchange(attended, "col", 1), exchange(passed, "col", 1))
    if last:
        expand_all, reduce_all = call(
            functools.partial(complete_kernel, [part[:2] for part in last], split),
            [shape((D, units), NARROW)] * 2, [VMEM] * (2 + len(last)), nbytes=2**22, limit=8,
        )(expand_all, reduce_all, *(part[2] for part in last))

    def mlp(offsets, *before):
        outs = [shape((TILE, D), NARROW if offset % 2 else WIDE) for offset in offsets]
        if 0 in offsets:
            outs.append(shape((TILE, D), NARROW))
        outs.append(mark)
        count = len(offsets) * TILE
        return call(
            functools.partial(mlp_kernel, offsets),
            outs,
            [SMEM] + [VMEM] * 9 + [ANYWHERE] * len(before),
            [pltpu.VMEM((count, D), NARROW)] * 2,
            flops=2 * count * D * (D + 2 * units), nbytes=8 * 2**20, trans=count * units, limit=20,
        )(table, *attended_blocks, tokens, terms, out_weight, expand_all, reduce_all, *before)

    tail = F.get("tail", 0)
    if tail == 3:
        far_kept, far_sent, near_sent, _ = mlp((2, 3, 1))
    else:
        far_kept, far_sent, far_done = mlp((2, 3))
    if tail == 0:
        near_sent, _ = mlp((1,), far_done)
    far_sum = (far_kept + exchange(far_sent, "col", 1).astype(WIDE)).astype(NARROW)
    crossed = exchange(far_sum, "col", 2)
    if tail == 1:
        near_sent, _ = mlp((1,), far_sum)
    if tail != 2:
        near_kept, residual, _ = mlp((0,), far_sum)
    else:
        near_kept, near_sent, residual, _ = mlp((0, 1), far_sum)
    beside = exchange(near_sent, "col", 1)
    noise = call(
        head_kernel,
        shape((TILE_ROWS, PATCH * IMG_WIDTH), WIDE),
        [SMEM] + [VMEM] * 6,
        flops=4 * TILE * D * IMG_WIDTH, nbytes=2**21, limit=8,
    )(table, near_kept, beside, crossed, residual, terms, head)

    noise_near = pack(noise, exchange(noise, "col", 1))
    img_rows = tiles * IMG_ROWS
    stepped, preview = call(
        step_kernel,
        [shape((img_rows, IMG_WIDTH), NARROW)] * 2,
        [SMEM] * 3 + [VMEM] * 4,
        [pltpu.VMEM((img_rows, IMG_WIDTH), WIDE)] * 2
        + [pltpu.VMEM((img_rows + 16, IMG_WIDTH), WIDE)] * 2,
        flops=12 * img_rows * IMG_WIDTH**2, nbytes=2**19,
    )(table, alpha_now, alpha_next, noise_near, exchange(noise_near, "col", 2), noisy_latent, bands)
    return (stepped, preview)


def solution(mesh):
    return jax.shard_map(
        shards,
        mesh=mesh,
        in_specs=(
            P("row", "col"),
            P("row", None),
            P(),
            P(),
            P(),
            P(),
            P(),
            P("row", None, "col"),
            P(None, None, "col"),
            P("col", None),
            P("row", "col"),
            P("col", "row"),
            P("col", None),
            P(),
        ),
        out_specs=(P("row", None), P("row", None)),
        check_vma=False,
    )
```

```python
import functools

import jax
import jax.numpy as jnp
from jax import lax
from jax.experimental import pallas as pl
from jax.experimental.pallas import tpu as pltpu
from jax.sharding import PartitionSpec as P

D = 1152
HEAD_DIM = 72
PATCH = 2
CHANNELS = 4
GRIDW = 16
NOISE = PATCH * PATCH * CHANNELS
TILE_ROWS = 8
STEPS = 50
TILE = 128
EPS_NORM = 1e-06
IMG_ROWS = TILE_ROWS * PATCH
IMG_WIDTH = GRIDW * PATCH * CHANNELS
WIDE = jnp.float32
NARROW = jnp.bfloat16
NT = (((1,), (1,)), ((), ()))
VMEM = pl.BlockSpec(memory_space=pltpu.VMEM)
SMEM = pl.BlockSpec(memory_space=pltpu.SMEM)
ANYWHERE = pl.BlockSpec(memory_space=pl.ANY)
MIB = 1024 * 1024


def call(kernel, outs, in_specs, scratch=(), flops=0, nbytes=0, trans=0, limit=4):
    return pl.pallas_call(
        kernel,
        out_shape=outs,
        in_specs=in_specs,
        out_specs=jax.tree.map(lambda _: VMEM, outs),
        scratch_shapes=list(scratch),
        compiler_params=pltpu.CompilerParams(vmem_limit_bytes=limit * MIB),
        cost_estimate=pl.CostEstimate(flops=flops, bytes_accessed=nbytes, transcendentals=trans),
    )


def exchange(value, axis, offset):
    size = lax.axis_size(axis)
    return lax.ppermute(value, axis, [(i, i ^ offset) for i in range(size)])


def after_kernel(*_):
    pass


def after(value, *before):
    return pl.pallas_call(
        after_kernel,
        out_shape=jax.ShapeDtypeStruct(value.shape, value.dtype),
        in_specs=[ANYWHERE] * (1 + len(before)),
        out_specs=ANYWHERE,
        input_output_aliases={0: 0},
        compiler_params=pltpu.CompilerParams(vmem_limit_bytes=MIB),
        cost_estimate=pl.CostEstimate(flops=0, bytes_accessed=0, transcendentals=0),
    )(value, *before)


def pack(first, second, *before):
    out = jax.ShapeDtypeStruct((2 * first.shape[0], first.shape[1]), first.dtype)
    return call(pair_kernel, out, [VMEM] * 2 + [ANYWHERE] * len(before), limit=8)(first, second, *before)


def normalize(values, shift_term, scale_term):
    mean_value = jnp.sum(values, axis=-1, keepdims=True) * (1.0 / D)
    spread = jnp.sum(values * values, axis=-1, keepdims=True) * (1.0 / D) - mean_value * mean_value
    normed = (values - mean_value) * lax.rsqrt(spread + EPS_NORM)
    return normed * (1.0 + scale_term) + shift_term


def condition_kernel(tiles_here, table_ref, embedding_ref, out_ref, mark_ref, onehot):
    count, depth = out_ref.shape
    tile_count = count // 2 * tiles_here
    mark_ref[...] = jnp.zeros(mark_ref.shape, WIDE)

    def pick(index, carry):
        tile = (index // 2) * tiles_here + (index % 2) * (tiles_here - 1)
        step = table_ref[tile_count + table_ref[tile]]
        lanes = lax.broadcasted_iota(jnp.int32, (1, STEPS), 1)
        onehot[pl.ds(index, 1), :] = jnp.where(lanes == step, 1.0, 0.0)
        return carry

    lax.fori_loop(0, count, pick, 0)
    embedded = jnp.dot(onehot[...].astype(NARROW), embedding_ref[...], preferred_element_type=WIDE)
    conditioning = (embedded / (1.0 + jnp.exp(-embedded))).astype(NARROW)
    first = lax.axis_index("row") * depth
    source = lax.broadcasted_iota(jnp.int32, (D, depth), 0)
    target = lax.broadcasted_iota(jnp.int32, (D, depth), 1) + first
    chosen = jnp.where(source == target, 1.0, 0.0).astype(NARROW)
    out_ref[...] = jnp.dot(conditioning, chosen, preferred_element_type=WIDE).astype(NARROW)


def tile_term(latent_ref, terms_ref, index, tile):
    first = lax.axis_index("row") * (lax.axis_size("col"))
    later = latent_ref[first + tile] != latent_ref[first]
    return jnp.where(later, terms_ref[8 + index : 9 + index, :], terms_ref[index : index + 1, :])


def pass_kernel(*refs):
    refs[-1][...] = refs[0][...]


def terms_kernel(terms_near, terms_far, terms_ref, columns):
    col = lax.axis_index("col")
    width = terms_near.shape[1]
    rows = terms_ref.shape[0]
    for place in range(4):

        @pl.when(col == place)
        def _():
            for offset in range(4):
                block = (terms_near, terms_far)[offset // 2]
                lower = (place ^ offset) * width
                terms_ref[:, lower : lower + width] = block[offset % 2 * rows : (offset % 2 + 1) * rows, :]

    columns[...] = terms_ref[...].T


def triple_kernel(latent_ref, own, beside, across, diagonal, columns, weight_ref, *refs):
    triple_ref, weight, weight_sem, normed = refs[-4:]
    fetch = pltpu.make_async_copy(weight_ref, weight, weight_sem)
    fetch.start()
    col = lax.axis_index("col")
    width, count = own.shape[0], triple_ref.shape[1]
    blocks = [source[:, :count] for source in (own, beside, across, diagonal)]
    total = jnp.zeros((1, count), WIDE)
    squares = jnp.zeros((1, count), WIDE)
    for block in blocks:
        values = block.astype(WIDE)
        total = total + jnp.sum(values, axis=0, keepdims=True)
        squares = squares + jnp.sum(values * values, axis=0, keepdims=True)
    mean_value = total * (1.0 / D)
    spread = squares * (1.0 / D) - mean_value * mean_value
    rate = lax.rsqrt(spread + EPS_NORM)
    first = lax.axis_index("row") * (count // TILE)
    later = [latent_ref[first + tile] != latent_ref[first] for tile in range(count // TILE)]
    for offset, block in enumerate(blocks):
        here = pl.ds(pl.multiple_of((col ^ offset) * width, 32), width)
        shifts = [jnp.broadcast_to(columns[here, at : at + 1], (width, TILE)) for at in (0, 8)]
        scales = [jnp.broadcast_to(columns[here, at : at + 1], (width, TILE)) + 1.0 for at in (1, 9)]
        for tile in range(count // TILE):
            lanes = slice(tile * TILE, (tile + 1) * TILE)
            values = (block[:, lanes].astype(WIDE) - mean_value[:, lanes]) * rate[:, lanes]
            scale = jnp.where(later[tile], scales[1], scales[0])
            shift = jnp.where(later[tile], shifts[1], shifts[0])
            normed[here, lanes] = (values * scale + shift).astype(NARROW)
    fetch.wait()
    triple_ref[...] = jnp.dot(weight[...], normed[...], preferred_element_type=WIDE)


def assemble_kernel(parts, depth, kernel_ref, own, beside, across, diagonal, *refs):
    pieces, (out_weight, expand, reduce, tokens_ref, head_ref, bands_ref) = refs[: len(parts)], refs[-6:]
    col = lax.axis_index("col")
    width, count = own.shape[0], tokens_ref.shape[0]
    for index, source in enumerate((own, across, beside, diagonal)):
        out_weight[index * width : (index + 1) * width, :] = source[:, count : count + D]
    for offset, source in enumerate((own, beside, across, diagonal)):
        head_ref[pl.ds(pl.multiple_of((col ^ offset) * width, 16), width), :] = source[:, count + D :]
    place_pieces(parts, depth, pieces, expand, reduce)
    for place in range(4):

        @pl.when(col == place)
        def _():
            for offset, source in enumerate((own, beside, across, diagonal)):
                lower = (place ^ offset) * width
                tokens_ref[:, lower : lower + width] = source[:, :count].T

    fill_bands(kernel_ref, bands_ref)


def attention_kernel(latent_ref, triple, *refs):
    attended_ref, mark_ref, mixed = refs[-3:]
    mark_ref[...] = jnp.zeros(mark_ref.shape, WIDE)
    row = lax.axis_index("row")
    width = attended_ref.shape[1]
    tiles = attended_ref.shape[0] // TILE
    latents = [latent_ref[row * tiles + tile] for tile in range(tiles)]
    factor = HEAD_DIM ** (-0.5) * 1.4426950408889634
    pair = 2
    for head in range(width // HEAD_DIM):
        lower = head * HEAD_DIM
        queries = triple[lower : lower + HEAD_DIM, :].astype(NARROW)
        keys = triple[width + lower : width + lower + HEAD_DIM, :].T.astype(NARROW)
        values = triple[2 * width + lower : 2 * width + lower + HEAD_DIM, :]
        values = jnp.concatenate([values, jnp.ones((8, values.shape[1]), WIDE)]).astype(NARROW)
        for first in range(0, tiles, pair):
            here = slice(first * TILE, (first + pair) * TILE)
            scores = jnp.dot(keys, queries[:, here], preferred_element_type=WIDE)
            columns = []
            for tile in range(first, first + pair):
                lanes = slice((tile - first) * TILE, (tile - first + 1) * TILE)
                blocks = [
                    scores[other * TILE : (other + 1) * TILE, lanes]
                    + jnp.where(latents[other] == latents[tile], 0.0, -1e30)
                    for other in range(tiles)
                ]
                peak = functools.reduce(jnp.maximum, blocks)
                peak = jnp.max(peak, axis=0, keepdims=True)
                raised = [jnp.exp2((block - peak) * factor).astype(NARROW) for block in blocks]
                columns.append(jnp.concatenate(raised, axis=0))
            summed = jnp.dot(values, jnp.concatenate(columns, axis=1), preferred_element_type=WIDE)
            mixed[lower : lower + HEAD_DIM, here] = summed[:HEAD_DIM] / summed[HEAD_DIM : HEAD_DIM + 1]
    attended_ref[...] = mixed[...].T.astype(NARROW)


def place_pieces(parts, depth, pieces, expand, reduce):
    row = lax.axis_index("row")
    for (offset, which), piece in zip(parts, pieces):
        start = pl.multiple_of((row ^ offset) * depth, 16) if depth < D else 0
        here = pl.ds(start, depth)
        if "e" in which:
            expand[here, :] = piece[:depth, :]
        if "r" in which:
            reduce[here, :] = piece[-depth:, :]


def complete_kernel(parts, depth, expand_before, reduce_before, *refs):
    pieces, (expand, reduce) = refs[:-2], refs[-2:]
    expand[...] = expand_before[...]
    reduce[...] = reduce_before[...]
    place_pieces(parts, depth, pieces, expand, reduce)


def pair_kernel(first, second, *refs):
    out_ref = refs[-1]
    count = first.shape[0]
    out_ref[:count, :] = first[...]
    out_ref[count:, :] = second[...]


def order_kernel(*refs):
    refs[-1][...] = jnp.zeros(refs[-1].shape, WIDE)


def shared_kernel(parts_ref, _, out_ref):
    out_ref[...] = jnp.sum(parts_ref[...], axis=0)


def mlp_kernel(
    offsets, latent_ref, att_own, att_across, att_beside, att_diagonal, tokens_ref, terms_ref, out_weight, expand, reduce, *refs
):
    outs, (mark_ref, attended, mid) = refs[-3 - len(offsets) - (0 in offsets) : -3], refs[-3:]
    mark_ref[...] = jnp.zeros(mark_ref.shape, WIDE)
    col = lax.axis_index("col")
    width = att_own.shape[1]
    tile_list = [col ^ offset for offset in offsets]
    starts = [pl.multiple_of(tile * TILE, TILE) for tile in tile_list]
    for place, block in enumerate((att_own, att_across, att_beside, att_diagonal)):
        for slot, start in enumerate(starts):
            here = slice(slot * TILE, (slot + 1) * TILE)
            attended[here, place * width : (place + 1) * width] = block[pl.ds(start, TILE), :]
    attn_sum = jnp.dot(attended[...], out_weight[...], preferred_element_type=WIDE)
    for slot, tile in enumerate(tile_list):
        term = functools.partial(tile_term, latent_ref, terms_ref, tile=tile)
        here = slice(slot * TILE, (slot + 1) * TILE)
        before = tokens_ref[pl.ds(starts[slot], TILE), :].astype(WIDE)
        residual = (before + term(2) * attn_sum[here]).astype(NARROW)
        if offsets[slot] == 0:
            outs[-1][...] = residual
        mid[here, :] = normalize(residual.astype(WIDE), term(3), term(4)).astype(NARROW)
    units = jnp.dot(mid[...], expand[...], preferred_element_type=WIDE)
    inner = 0.7978845608028654 * (units + 0.044715 * (units * units * units))
    activated = (0.5 * units * (1.0 + jnp.tanh(inner))).astype(NARROW)
    summed = lax.dot_general(activated, reduce[...], NT, preferred_element_type=WIDE)
    for slot, out in enumerate(outs[: len(offsets)]):
        out[...] = summed[slot * TILE : (slot + 1) * TILE].astype(out.dtype)


def head_kernel(latent_ref, kept_ref, beside_ref, crossed_ref, residual_ref, terms_ref, head_ref, out_ref):
    col = lax.axis_index("col")
    term = functools.partial(tile_term, latent_ref, terms_ref, tile=col)
    mlp_sum = kept_ref[...] + beside_ref[...].astype(WIDE) + crossed_ref[...].astype(WIDE)
    second = (residual_ref[...].astype(WIDE) + term(5) * mlp_sum).astype(NARROW).astype(WIDE)
    normed = normalize(second, term(6), term(7)).astype(NARROW)
    group = PATCH * CHANNELS
    token_place = lax.broadcasted_iota(jnp.int32, (TILE, IMG_WIDTH), 0) % GRIDW
    lane_place = lax.broadcasted_iota(jnp.int32, (TILE, IMG_WIDTH), 1) // group
    source = lax.broadcasted_iota(jnp.int32, (NOISE, PATCH * IMG_WIDTH), 0)
    target = lax.broadcasted_iota(jnp.int32, (NOISE, PATCH * IMG_WIDTH), 1)
    chosen = jnp.where(source == target // IMG_WIDTH * group + target % group, 1.0, 0.0).astype(NARROW)
    spread_head = jnp.dot(head_ref[...], chosen, preferred_element_type=WIDE).astype(NARROW)
    noise = jnp.dot(normed, spread_head, preferred_element_type=WIDE)
    for dy in range(PATCH):
        lanes = slice(dy * IMG_WIDTH, (dy + 1) * IMG_WIDTH)
        kept = jnp.where(token_place == lane_place, noise[:, lanes], 0.0)
        out_ref[:, lanes] = jnp.sum(kept.reshape(TILE_ROWS, GRIDW, IMG_WIDTH), axis=1)


def fill_bands(kernel_ref, out_ref):
    shape = (IMG_WIDTH, IMG_WIDTH)
    source = lax.broadcasted_iota(jnp.int32, shape, 0)
    target = lax.broadcasted_iota(jnp.int32, shape, 1)
    reach = 3 * CHANNELS
    apart = target - (source // CHANNELS) * CHANNELS + CHANNELS
    code = jnp.where((apart >= 0) & (apart < reach), (source % CHANNELS) * reach + apart, -1)
    bands = [jnp.zeros(shape, WIDE) for _ in range(3)]
    for channel in range(CHANNELS):
        for lane in range(reach):
            here = code == channel * reach + lane
            column, out_channel = 2 - lane // CHANNELS, lane % CHANNELS
            for line in range(3):
                value = kernel_ref[line, column, channel, out_channel]
                bands[line] = jnp.where(here, value, bands[line])
    for line in range(3):
        out_ref[:, line * IMG_WIDTH : (line + 1) * IMG_WIDTH] = bands[line]


def step_kernel(
    table_ref, now_ref, next_ref, near, far, noisy_ref, bands_ref,
    stepped_ref, preview_ref, image, clean, above, below,
):
    tiles = noisy_ref.shape[0] // IMG_ROWS
    row = lax.axis_index("row")
    tile_count = lax.axis_size("row") * tiles
    col = lax.axis_index("col")
    for place in range(4):

        @pl.when(col == place)
        def _():
            for offset in range(4):
                block = (near, far)[offset // 2]
                rows = slice(offset % 2 * TILE_ROWS, (offset % 2 + 1) * TILE_ROWS)
                for dy in range(PATCH):
                    start = (place ^ offset) * IMG_ROWS + dy
                    image[pl.ds(start, TILE_ROWS, PATCH), :] = block[rows, dy * IMG_WIDTH : (dy + 1) * IMG_WIDTH]

    for tile in range(tiles):
        here = slice(tile * IMG_ROWS, (tile + 1) * IMG_ROWS)
        step = table_ref[tile_count + table_ref[row * tiles + tile]]
        signal_now = jnp.full((1, IMG_WIDTH), now_ref[step], WIDE)
        signal_next = jnp.full((1, IMG_WIDTH), next_ref[step], WIDE)
        noise = image[here, :]
        rows = (noisy_ref[here, :].astype(WIDE) - jnp.sqrt(1.0 - signal_now) * noise) / jnp.sqrt(signal_now)
        clean[here, :] = rows
        stepped = jnp.sqrt(signal_next) * rows + jnp.sqrt(1.0 - signal_next) * noise
        stepped_ref[here, :] = stepped.astype(NARROW)
    parts = jnp.dot(
        clean[...], bands_ref[...], precision=lax.Precision.HIGHEST, preferred_element_type=WIDE
    )
    count = tiles * IMG_ROWS
    above[8 : 8 + count, :] = parts[:, :IMG_WIDTH]
    below[8 : 8 + count, :] = parts[:, 2 * IMG_WIDTH :]
    for tile in range(tiles):
        here = slice(tile * IMG_ROWS, (tile + 1) * IMG_ROWS)
        start = 8 + tile * IMG_ROWS
        line = lax.broadcasted_iota(jnp.int32, (IMG_ROWS, IMG_WIDTH), 0)
        from_above = above[start - 1 : start - 1 + IMG_ROWS, :]
        from_below = below[start + 1 : start + 1 + IMG_ROWS, :]
        mine = table_ref[row * tiles + tile]
        if tile == 0:
            above_ok = line > 0
        else:
            above_ok = (line > 0) | (table_ref[row * tiles + tile - 1] == mine)
        if tile == tiles - 1:
            below_ok = line < IMG_ROWS - 1
        else:
            below_ok = (line < IMG_ROWS - 1) | (table_ref[row * tiles + tile + 1] == mine)
        total = parts[here, IMG_WIDTH : 2 * IMG_WIDTH]
        total = total + jnp.where(above_ok, from_above, 0.0) + jnp.where(below_ok, from_below, 0.0)
        preview_ref[here, :] = total.astype(NARROW)


def shards(
    hidden,
    noisy_latent,
    tile_latent,
    timesteps,
    step_embedding,
    alpha_now,
    alpha_next,
    modulation,
    attention_in,
    attention_out,
    expand_weight,
    reduce_weight,
    noise_head,
    preview_kernel,
):
    rows = lax.axis_size("row")
    tokens_here, width = hidden.shape
    tiles = tokens_here // TILE
    depth = modulation.shape[0]
    units = expand_weight.shape[1]
    shape = jax.ShapeDtypeStruct

    table = jnp.concatenate([tile_latent, timesteps])
    mark = shape((8, 128), WIDE)
    conditioning, conditioned = call(
        functools.partial(condition_kernel, tiles),
        [shape((2 * rows, depth), NARROW), mark],
        [SMEM, VMEM],
        [pltpu.VMEM((2 * rows, STEPS), WIDE)],
        flops=2 * 2 * rows * D * (STEPS + depth), nbytes=2 * STEPS * D,
    )(table, step_embedding)
    partial = jnp.einsum("td,dkc->tkc", conditioning, modulation, preferred_element_type=WIDE)
    partial = partial.reshape(rows, 16, width)
    received = lax.all_to_all(partial, "row", 0, 0, tiled=True)
    blocks_here = jnp.concatenate([hidden.T, attention_out, noise_head], axis=1)
    blocks_across = exchange(blocks_here, "col", 2)
    reduce_rows = reduce_weight.T
    staged = rows == 8
    if staged:
        both = jnp.concatenate([expand_weight, reduce_rows], axis=0)
        both_4 = exchange(both, "row", 4)
        both_2 = exchange(both, "row", 2)
        both_1 = exchange(both, "row", 1)
        first = [both_4, both_2, both_1]
    else:
        expand_whole = lax.all_gather(expand_weight, "row", axis=0, tiled=True)
        reduce_whole = lax.all_gather(reduce_rows, "row", axis=0, tiled=True)
        first = []
    arrived = call(order_kernel, mark, [ANYWHERE] * (1 + len(first)))(conditioned, *first)
    shared = call(shared_kernel, shape((16, width), WIDE), [VMEM, ANYWHERE], nbytes=2**18)(received, arrived)
    if staged:
        both_3 = exchange(both_2, "row", 1)
        both_6 = exchange(both_4, "row", 2)
        both_5 = exchange(both_4, "row", 1)
        both_7 = exchange(both_5, "row", 2)
        parts = [(0, "er", both), (1, "er", both_1), (2, "er", both_2), (4, "er", both_4), (5, "er", both_5), (6, "er", both_6)]
        parts.append((3, "er", both_3))
        last = [(7, "er", both_7)]
    else:
        parts, last = [(0, "e", expand_whole), (0, "r", reduce_whole)], []
    terms_near = pack(shared, exchange(shared, "col", 1))
    terms_far = exchange(terms_near, "col", 2)
    blocks_across = after(blocks_across, terms_near)
    blocks = (blocks_here, exchange(blocks_here, "col", 1), blocks_across, exchange(blocks_across, "col", 1))
    attention_weight = attention_in.transpose(1, 2, 0).reshape(3 * width, D)
    terms, columns = call(
        terms_kernel, [shape((16, D), WIDE), shape((D, 16), WIDE)], [VMEM] * 2, flops=4 * 10**9
    )(terms_near, terms_far)
    triple = call(
        triple_kernel,
        shape((3 * width, tokens_here), WIDE),
        [SMEM] + [VMEM] * 5 + [ANYWHERE],
        [
            pltpu.VMEM((3 * width, D), NARROW),
            pltpu.SemaphoreType.DMA,
            pltpu.VMEM((D, tokens_here), NARROW),
        ],
        flops=2 * tokens_here * D * 3 * width, nbytes=5 * 2**20, limit=16,
    )(table, *blocks, columns, attention_weight)
    attended, attention_done = call(
        attention_kernel,
        [shape((tokens_here, width), NARROW), mark],
        [SMEM, VMEM],
        [pltpu.VMEM((width, tokens_here), WIDE)],
        flops=4 * tokens_here * tokens_here * width, trans=4 * tokens_here**2, limit=16,
    )(table, triple)
    split = depth if staged else D
    out_weight, expand_all, reduce_all, tokens, head, bands = call(
        functools.partial(assemble_kernel, [part[:2] for part in parts], split),
        [
            shape((D, D), NARROW),
            shape((D, units), NARROW),
            shape((D, units), NARROW),
            shape((tokens_here, D), NARROW),
            shape((D, NOISE), NARROW),
            shape((IMG_WIDTH, 3 * IMG_WIDTH), WIDE),
        ],
        [SMEM] + [VMEM] * (4 + len(parts)) + [ANYWHERE],
        nbytes=2**23, limit=24,
    )(preview_kernel, *blocks, *(part[2] for part in parts), attention_done)
    if staged:
        attended = after(attended, both_6)
    across = exchange(attended, "col", 2)
    passed = call(pass_kernel, shape(across.shape, NARROW), [VMEM, ANYWHERE], nbytes=2**19)(across, tokens)
    attended_blocks = (attended, across, exchange(attended, "col", 1), exchange(passed, "col", 1))
    if last:
        expand_all, reduce_all = call(
            functools.partial(complete_kernel, [part[:2] for part in last], split),
            [shape((D, units), NARROW)] * 2, [VMEM] * (2 + len(last)), nbytes=2**22, limit=8,
        )(expand_all, reduce_all, *(part[2] for part in last))

    def mlp(offsets, *before):
        outs = [shape((TILE, D), NARROW if offset % 2 else WIDE) for offset in offsets]
        if 0 in offsets:
            outs.append(shape((TILE, D), NARROW))
        outs.append(mark)
        count = len(offsets) * TILE
        return call(
            functools.partial(mlp_kernel, offsets),
            outs,
            [SMEM] + [VMEM] * 9 + [ANYWHERE] * len(before),
            [pltpu.VMEM((count, D), NARROW)] * 2,
            flops=2 * count * D * (D + 2 * units), nbytes=8 * 2**20, trans=count * units, limit=20,
        )(table, *attended_blocks, tokens, terms, out_weight, expand_all, reduce_all, *before)

    far_kept, far_sent, far_done = mlp((2, 3))
    near_sent, _ = mlp((1,), far_done)
    far_sum = (far_kept + exchange(far_sent, "col", 1).astype(WIDE)).astype(NARROW)
    crossed = exchange(far_sum, "col", 2)
    near_kept, residual, _ = mlp((0,), far_sum)
    beside = exchange(near_sent, "col", 1)
    noise = call(
        head_kernel,
        shape((TILE_ROWS, PATCH * IMG_WIDTH), WIDE),
        [SMEM] + [VMEM] * 6,
        flops=4 * TILE * D * IMG_WIDTH, nbytes=2**21, limit=8,
    )(table, near_kept, beside, crossed, residual, terms, head)

    noise_near = pack(noise, exchange(noise, "col", 1))
    img_rows = tiles * IMG_ROWS
    stepped, preview = call(
        step_kernel,
        [shape((img_rows, IMG_WIDTH), NARROW)] * 2,
        [SMEM] * 3 + [VMEM] * 4,
        [pltpu.VMEM((img_rows, IMG_WIDTH), WIDE)] * 2
        + [pltpu.VMEM((img_rows + 16, IMG_WIDTH), WIDE)] * 2,
        flops=12 * img_rows * IMG_WIDTH**2, nbytes=2**19,
    )(table, alpha_now, alpha_next, noise_near, exchange(noise_near, "col", 2), noisy_latent, bands)
    return (stepped, preview)


def solution(mesh):
    return jax.shard_map(
        shards,
        mesh=mesh,
        in_specs=(
            P("row", "col"),
            P("row", None),
            P(),
            P(),
            P(),
            P(),
            P(),
            P("row", None, "col"),
            P(None, None, "col"),
            P("col", None),
            P("row", "col"),
            P("col", "row"),
            P("col", None),
            P(),
        ),
        out_specs=(P("row", None), P("row", None)),
        check_vma=False,
    )
```

```python
import functools

import jax
import jax.numpy as jnp
from jax import lax
from jax.experimental import pallas as pl
from jax.experimental.pallas import tpu as pltpu
from jax.sharding import PartitionSpec as P

D = 1152
HEAD_DIM = 72
PATCH = 2
CHANNELS = 4
GRIDW = 16
NOISE = PATCH * PATCH * CHANNELS
TILE_ROWS = 8
STEPS = 50
TILE = 128
EPS_NORM = 1e-06
IMG_ROWS = TILE_ROWS * PATCH
IMG_WIDTH = GRIDW * PATCH * CHANNELS
WIDE = jnp.float32
NARROW = jnp.bfloat16
NT = (((1,), (1,)), ((), ()))
VMEM = pl.BlockSpec(memory_space=pltpu.VMEM)
SMEM = pl.BlockSpec(memory_space=pltpu.SMEM)
ANYWHERE = pl.BlockSpec(memory_space=pl.ANY)
MIB = 1024 * 1024


def call(kernel, outs, in_specs, scratch=(), flops=0, nbytes=0, trans=0, limit=4):
    return pl.pallas_call(
        kernel,
        out_shape=outs,
        in_specs=in_specs,
        out_specs=jax.tree.map(lambda _: VMEM, outs),
        scratch_shapes=list(scratch),
        compiler_params=pltpu.CompilerParams(vmem_limit_bytes=limit * MIB),
        cost_estimate=pl.CostEstimate(flops=flops, bytes_accessed=nbytes, transcendentals=trans),
    )


def exchange(value, axis, offset):
    size = lax.axis_size(axis)
    return lax.ppermute(value, axis, [(i, i ^ offset) for i in range(size)])


def after_kernel(*_):
    pass


def after(value, *before):
    return pl.pallas_call(
        after_kernel,
        out_shape=jax.ShapeDtypeStruct(value.shape, value.dtype),
        in_specs=[ANYWHERE] * (1 + len(before)),
        out_specs=ANYWHERE,
        input_output_aliases={0: 0},
        compiler_params=pltpu.CompilerParams(vmem_limit_bytes=MIB),
        cost_estimate=pl.CostEstimate(flops=0, bytes_accessed=0, transcendentals=0),
    )(value, *before)


def pack(first, second, *before):
    out = jax.ShapeDtypeStruct((2 * first.shape[0], first.shape[1]), first.dtype)
    return call(pair_kernel, out, [VMEM] * 2 + [ANYWHERE] * len(before), limit=8)(first, second, *before)


def normalize(values, shift_term, scale_term):
    mean_value = jnp.sum(values, axis=-1, keepdims=True) * (1.0 / D)
    spread = jnp.sum(values * values, axis=-1, keepdims=True) * (1.0 / D) - mean_value * mean_value
    normed = (values - mean_value) * lax.rsqrt(spread + EPS_NORM)
    return normed * (1.0 + scale_term) + shift_term


def condition_kernel(tiles_here, table_ref, embedding_ref, out_ref, mark_ref, onehot):
    count, depth = out_ref.shape
    tile_count = count // 2 * tiles_here
    mark_ref[...] = jnp.zeros(mark_ref.shape, WIDE)

    def pick(index, carry):
        tile = (index // 2) * tiles_here + (index % 2) * (tiles_here - 1)
        step = table_ref[tile_count + table_ref[tile]]
        lanes = lax.broadcasted_iota(jnp.int32, (1, STEPS), 1)
        onehot[pl.ds(index, 1), :] = jnp.where(lanes == step, 1.0, 0.0)
        return carry

    lax.fori_loop(0, count, pick, 0)
    embedded = jnp.dot(onehot[...].astype(NARROW), embedding_ref[...], preferred_element_type=WIDE)
    conditioning = (embedded / (1.0 + jnp.exp(-embedded))).astype(NARROW)
    first = lax.axis_index("row") * depth
    source = lax.broadcasted_iota(jnp.int32, (D, depth), 0)
    target = lax.broadcasted_iota(jnp.int32, (D, depth), 1) + first
    chosen = jnp.where(source == target, 1.0, 0.0).astype(NARROW)
    out_ref[...] = jnp.dot(conditioning, chosen, preferred_element_type=WIDE).astype(NARROW)


def tile_term(latent_ref, terms_ref, index, tile):
    first = lax.axis_index("row") * (lax.axis_size("col"))
    later = latent_ref[first + tile] != latent_ref[first]
    return jnp.where(later, terms_ref[8 + index : 9 + index, :], terms_ref[index : index + 1, :])


def terms_kernel(terms_near, terms_far, terms_ref, columns):
    col = lax.axis_index("col")
    width = terms_near.shape[1]
    rows = terms_ref.shape[0]
    for place in range(4):

        @pl.when(col == place)
        def _():
            for offset in range(4):
                block = (terms_near, terms_far)[offset // 2]
                lower = (place ^ offset) * width
                terms_ref[:, lower : lower + width] = block[offset % 2 * rows : (offset % 2 + 1) * rows, :]

    columns[...] = terms_ref[...].T


def triple_kernel(latent_ref, own, beside, across, diagonal, columns, weight_ref, *refs):
    triple_ref, weight, weight_sem, normed = refs[-4:]
    fetch = pltpu.make_async_copy(weight_ref, weight, weight_sem)
    fetch.start()
    col = lax.axis_index("col")
    width, count = own.shape[0], triple_ref.shape[1]
    blocks = [source[:, :count] for source in (own, beside, across, diagonal)]
    total = jnp.zeros((1, count), WIDE)
    squares = jnp.zeros((1, count), WIDE)
    for block in blocks:
        values = block.astype(WIDE)
        total = total + jnp.sum(values, axis=0, keepdims=True)
        squares = squares + jnp.sum(values * values, axis=0, keepdims=True)
    mean_value = total * (1.0 / D)
    spread = squares * (1.0 / D) - mean_value * mean_value
    rate = lax.rsqrt(spread + EPS_NORM)
    first = lax.axis_index("row") * (count // TILE)
    later = [latent_ref[first + tile] != latent_ref[first] for tile in range(count // TILE)]
    for offset, block in enumerate(blocks):
        here = pl.ds(pl.multiple_of((col ^ offset) * width, 32), width)
        shifts = [jnp.broadcast_to(columns[here, at : at + 1], (width, TILE)) for at in (0, 8)]
        scales = [jnp.broadcast_to(columns[here, at : at + 1], (width, TILE)) + 1.0 for at in (1, 9)]
        for tile in range(count // TILE):
            lanes = slice(tile * TILE, (tile + 1) * TILE)
            values = (block[:, lanes].astype(WIDE) - mean_value[:, lanes]) * rate[:, lanes]
            scale = jnp.where(later[tile], scales[1], scales[0])
            shift = jnp.where(later[tile], shifts[1], shifts[0])
            normed[here, lanes] = (values * scale + shift).astype(NARROW)
    fetch.wait()
    triple_ref[...] = jnp.dot(weight[...], normed[...], preferred_element_type=WIDE)


def assemble_kernel(parts, depth, kernel_ref, own, beside, across, diagonal, *refs):
    pieces, (out_weight, expand, reduce, tokens_ref, head_ref, bands_ref) = refs[: len(parts)], refs[-6:]
    col = lax.axis_index("col")
    width, count = own.shape[0], tokens_ref.shape[0]
    for index, source in enumerate((own, across, beside, diagonal)):
        out_weight[index * width : (index + 1) * width, :] = source[:, count : count + D]
    for offset, source in enumerate((own, beside, across, diagonal)):
        head_ref[pl.ds(pl.multiple_of((col ^ offset) * width, 16), width), :] = source[:, count + D :]
    place_pieces(parts, depth, pieces, expand, reduce)
    for place in range(4):

        @pl.when(col == place)
        def _():
            for offset, source in enumerate((own, beside, across, diagonal)):
                lower = (place ^ offset) * width
                tokens_ref[:, lower : lower + width] = source[:, :count].T

    fill_bands(kernel_ref, bands_ref)


def attention_kernel(latent_ref, triple, *refs):
    attended_ref, mark_ref, mixed = refs[-3:]
    mark_ref[...] = jnp.zeros(mark_ref.shape, WIDE)
    row = lax.axis_index("row")
    width = attended_ref.shape[1]
    tiles = attended_ref.shape[0] // TILE
    latents = [latent_ref[row * tiles + tile] for tile in range(tiles)]
    factor = HEAD_DIM ** (-0.5) * 1.4426950408889634
    pair = 2
    for head in range(width // HEAD_DIM):
        lower = head * HEAD_DIM
        queries = triple[lower : lower + HEAD_DIM, :].astype(NARROW)
        keys = triple[width + lower : width + lower + HEAD_DIM, :].T.astype(NARROW)
        values = triple[2 * width + lower : 2 * width + lower + HEAD_DIM, :]
        values = jnp.concatenate([values, jnp.ones((8, values.shape[1]), WIDE)]).astype(NARROW)
        for first in range(0, tiles, pair):
            here = slice(first * TILE, (first + pair) * TILE)
            scores = jnp.dot(keys, queries[:, here], preferred_element_type=WIDE)
            columns = []
            for tile in range(first, first + pair):
                lanes = slice((tile - first) * TILE, (tile - first + 1) * TILE)
                blocks = [
                    scores[other * TILE : (other + 1) * TILE, lanes]
                    + jnp.where(latents[other] == latents[tile], 0.0, -1e30)
                    for other in range(tiles)
                ]
                peak = functools.reduce(jnp.maximum, blocks)
                peak = jnp.max(peak, axis=0, keepdims=True)
                raised = [jnp.exp2((block - peak) * factor).astype(NARROW) for block in blocks]
                columns.append(jnp.concatenate(raised, axis=0))
            summed = jnp.dot(values, jnp.concatenate(columns, axis=1), preferred_element_type=WIDE)
            mixed[lower : lower + HEAD_DIM, here] = summed[:HEAD_DIM] / summed[HEAD_DIM : HEAD_DIM + 1]
    attended_ref[...] = mixed[...].T.astype(NARROW)


def place_pieces(parts, depth, pieces, expand, reduce):
    row = lax.axis_index("row")
    for (offset, which), piece in zip(parts, pieces):
        start = pl.multiple_of((row ^ offset) * depth, 16) if depth < D else 0
        here = pl.ds(start, depth)
        if "e" in which:
            expand[here, :] = piece[:depth, :]
        if "r" in which:
            reduce[here, :] = piece[-depth:, :]


def complete_kernel(parts, depth, expand_before, reduce_before, *refs):
    pieces, (expand, reduce) = refs[:-2], refs[-2:]
    expand[...] = expand_before[...]
    reduce[...] = reduce_before[...]
    place_pieces(parts, depth, pieces, expand, reduce)


def pair_kernel(first, second, *refs):
    out_ref = refs[-1]
    count = first.shape[0]
    out_ref[:count, :] = first[...]
    out_ref[count:, :] = second[...]


def order_kernel(*refs):
    refs[-1][...] = jnp.zeros(refs[-1].shape, WIDE)


def shared_kernel(parts_ref, _, out_ref):
    out_ref[...] = jnp.sum(parts_ref[...], axis=0)


def mlp_kernel(
    offsets, latent_ref, att_own, att_across, att_beside, att_diagonal, tokens_ref, terms_ref, out_weight, expand, reduce, *refs
):
    outs, (mark_ref, attended, mid) = refs[-3 - len(offsets) - (0 in offsets) : -3], refs[-3:]
    mark_ref[...] = jnp.zeros(mark_ref.shape, WIDE)
    col = lax.axis_index("col")
    width = att_own.shape[1]
    tile_list = [col ^ offset for offset in offsets]
    starts = [pl.multiple_of(tile * TILE, TILE) for tile in tile_list]
    for place, block in enumerate((att_own, att_across, att_beside, att_diagonal)):
        for slot, start in enumerate(starts):
            here = slice(slot * TILE, (slot + 1) * TILE)
            attended[here, place * width : (place + 1) * width] = block[pl.ds(start, TILE), :]
    attn_sum = jnp.dot(attended[...], out_weight[...], preferred_element_type=WIDE)
    for slot, tile in enumerate(tile_list):
        term = functools.partial(tile_term, latent_ref, terms_ref, tile=tile)
        here = slice(slot * TILE, (slot + 1) * TILE)
        before = tokens_ref[pl.ds(starts[slot], TILE), :].astype(WIDE)
        residual = (before + term(2) * attn_sum[here]).astype(NARROW)
        if offsets[slot] == 0:
            outs[-1][...] = residual
        mid[here, :] = normalize(residual.astype(WIDE), term(3), term(4)).astype(NARROW)
    units = jnp.dot(mid[...], expand[...], preferred_element_type=WIDE)
    inner = 0.7978845608028654 * (units + 0.044715 * (units * units * units))
    activated = (0.5 * units * (1.0 + jnp.tanh(inner))).astype(NARROW)
    summed = lax.dot_general(activated, reduce[...], NT, preferred_element_type=WIDE)
    for slot, out in enumerate(outs[: len(offsets)]):
        out[...] = summed[slot * TILE : (slot + 1) * TILE].astype(out.dtype)


def head_kernel(latent_ref, kept_ref, beside_ref, crossed_ref, residual_ref, terms_ref, head_ref, out_ref):
    col = lax.axis_index("col")
    term = functools.partial(tile_term, latent_ref, terms_ref, tile=col)
    mlp_sum = kept_ref[...] + beside_ref[...].astype(WIDE) + crossed_ref[...].astype(WIDE)
    second = (residual_ref[...].astype(WIDE) + term(5) * mlp_sum).astype(NARROW).astype(WIDE)
    normed = normalize(second, term(6), term(7)).astype(NARROW)
    group = PATCH * CHANNELS
    token_place = lax.broadcasted_iota(jnp.int32, (TILE, IMG_WIDTH), 0) % GRIDW
    lane_place = lax.broadcasted_iota(jnp.int32, (TILE, IMG_WIDTH), 1) // group
    source = lax.broadcasted_iota(jnp.int32, (NOISE, PATCH * IMG_WIDTH), 0)
    target = lax.broadcasted_iota(jnp.int32, (NOISE, PATCH * IMG_WIDTH), 1)
    chosen = jnp.where(source == target // IMG_WIDTH * group + target % group, 1.0, 0.0).astype(NARROW)
    spread_head = jnp.dot(head_ref[...], chosen, preferred_element_type=WIDE).astype(NARROW)
    noise = jnp.dot(normed, spread_head, preferred_element_type=WIDE)
    for dy in range(PATCH):
        lanes = slice(dy * IMG_WIDTH, (dy + 1) * IMG_WIDTH)
        kept = jnp.where(token_place == lane_place, noise[:, lanes], 0.0)
        out_ref[:, lanes] = jnp.sum(kept.reshape(TILE_ROWS, GRIDW, IMG_WIDTH), axis=1)


def fill_bands(kernel_ref, out_ref):
    shape = (IMG_WIDTH, IMG_WIDTH)
    source = lax.broadcasted_iota(jnp.int32, shape, 0)
    target = lax.broadcasted_iota(jnp.int32, shape, 1)
    reach = 3 * CHANNELS
    apart = target - (source // CHANNELS) * CHANNELS + CHANNELS
    code = jnp.where((apart >= 0) & (apart < reach), (source % CHANNELS) * reach + apart, -1)
    bands = [jnp.zeros(shape, WIDE) for _ in range(3)]
    for channel in range(CHANNELS):
        for lane in range(reach):
            here = code == channel * reach + lane
            column, out_channel = 2 - lane // CHANNELS, lane % CHANNELS
            for line in range(3):
                value = kernel_ref[line, column, channel, out_channel]
                bands[line] = jnp.where(here, value, bands[line])
    for line in range(3):
        out_ref[:, line * IMG_WIDTH : (line + 1) * IMG_WIDTH] = bands[line]


def step_kernel(
    table_ref, now_ref, next_ref, near, far, noisy_ref, bands_ref,
    stepped_ref, preview_ref, image, clean, above, below,
):
    tiles = noisy_ref.shape[0] // IMG_ROWS
    row = lax.axis_index("row")
    tile_count = lax.axis_size("row") * tiles
    col = lax.axis_index("col")
    for place in range(4):

        @pl.when(col == place)
        def _():
            for offset in range(4):
                block = (near, far)[offset // 2]
                rows = slice(offset % 2 * TILE_ROWS, (offset % 2 + 1) * TILE_ROWS)
                for dy in range(PATCH):
                    start = (place ^ offset) * IMG_ROWS + dy
                    image[pl.ds(start, TILE_ROWS, PATCH), :] = block[rows, dy * IMG_WIDTH : (dy + 1) * IMG_WIDTH]

    for tile in range(tiles):
        here = slice(tile * IMG_ROWS, (tile + 1) * IMG_ROWS)
        step = table_ref[tile_count + table_ref[row * tiles + tile]]
        signal_now = jnp.full((1, IMG_WIDTH), now_ref[step], WIDE)
        signal_next = jnp.full((1, IMG_WIDTH), next_ref[step], WIDE)
        noise = image[here, :]
        rows = (noisy_ref[here, :].astype(WIDE) - jnp.sqrt(1.0 - signal_now) * noise) / jnp.sqrt(signal_now)
        clean[here, :] = rows
        stepped = jnp.sqrt(signal_next) * rows + jnp.sqrt(1.0 - signal_next) * noise
        stepped_ref[here, :] = stepped.astype(NARROW)
    parts = jnp.dot(
        clean[...], bands_ref[...], precision=lax.Precision.HIGHEST, preferred_element_type=WIDE
    )
    count = tiles * IMG_ROWS
    above[8 : 8 + count, :] = parts[:, :IMG_WIDTH]
    below[8 : 8 + count, :] = parts[:, 2 * IMG_WIDTH :]
    for tile in range(tiles):
        here = slice(tile * IMG_ROWS, (tile + 1) * IMG_ROWS)
        start = 8 + tile * IMG_ROWS
        line = lax.broadcasted_iota(jnp.int32, (IMG_ROWS, IMG_WIDTH), 0)
        from_above = above[start - 1 : start - 1 + IMG_ROWS, :]
        from_below = below[start + 1 : start + 1 + IMG_ROWS, :]
        mine = table_ref[row * tiles + tile]
        if tile == 0:
            above_ok = line > 0
        else:
            above_ok = (line > 0) | (table_ref[row * tiles + tile - 1] == mine)
        if tile == tiles - 1:
            below_ok = line < IMG_ROWS - 1
        else:
            below_ok = (line < IMG_ROWS - 1) | (table_ref[row * tiles + tile + 1] == mine)
        total = parts[here, IMG_WIDTH : 2 * IMG_WIDTH]
        total = total + jnp.where(above_ok, from_above, 0.0) + jnp.where(below_ok, from_below, 0.0)
        preview_ref[here, :] = total.astype(NARROW)


def shards(
    hidden,
    noisy_latent,
    tile_latent,
    timesteps,
    step_embedding,
    alpha_now,
    alpha_next,
    modulation,
    attention_in,
    attention_out,
    expand_weight,
    reduce_weight,
    noise_head,
    preview_kernel,
):
    rows = lax.axis_size("row")
    tokens_here, width = hidden.shape
    tiles = tokens_here // TILE
    depth = modulation.shape[0]
    units = expand_weight.shape[1]
    shape = jax.ShapeDtypeStruct

    table = jnp.concatenate([tile_latent, timesteps])
    mark = shape((8, 128), WIDE)
    conditioning, conditioned = call(
        functools.partial(condition_kernel, tiles),
        [shape((2 * rows, depth), NARROW), mark],
        [SMEM, VMEM],
        [pltpu.VMEM((2 * rows, STEPS), WIDE)],
        flops=2 * 2 * rows * D * (STEPS + depth), nbytes=2 * STEPS * D,
    )(table, step_embedding)
    partial = jnp.einsum("td,dkc->tkc", conditioning, modulation, preferred_element_type=WIDE)
    partial = partial.reshape(rows, 16, width)
    received = lax.all_to_all(partial, "row", 0, 0, tiled=True)
    blocks_here = jnp.concatenate([hidden.T, attention_out, noise_head], axis=1)
    blocks_across = exchange(blocks_here, "col", 2)
    reduce_rows = reduce_weight.T
    staged = rows == 8
    if staged:
        both = jnp.concatenate([expand_weight, reduce_rows], axis=0)
        both_4 = exchange(both, "row", 4)
        both_2 = exchange(both, "row", 2)
        both_1 = exchange(both, "row", 1)
        first = [both_4, both_2, both_1]
    else:
        expand_whole = lax.all_gather(expand_weight, "row", axis=0, tiled=True)
        reduce_whole = lax.all_gather(reduce_rows, "row", axis=0, tiled=True)
        first = []
    arrived = call(order_kernel, mark, [ANYWHERE] * (1 + len(first)))(conditioned, *first)
    shared = call(shared_kernel, shape((16, width), WIDE), [VMEM, ANYWHERE], nbytes=2**18)(received, arrived)
    if staged:
        both_3 = exchange(both_2, "row", 1)
        both_6 = exchange(both_4, "row", 2)
        both_5 = exchange(both_4, "row", 1)
        both_7 = exchange(both_5, "row", 2)
        parts = [(0, "er", both), (1, "er", both_1), (2, "er", both_2), (4, "er", both_4), (5, "er", both_5), (6, "er", both_6)]
        parts.append((3, "er", both_3))
        last = [(7, "er", both_7)]
    else:
        parts, last = [(0, "e", expand_whole), (0, "r", reduce_whole)], []
    terms_near = pack(shared, exchange(shared, "col", 1))
    terms_far = exchange(terms_near, "col", 2)
    blocks_across = after(blocks_across, terms_near)
    blocks = (blocks_here, exchange(blocks_here, "col", 1), blocks_across, exchange(blocks_across, "col", 1))
    attention_weight = attention_in.transpose(1, 2, 0).reshape(3 * width, D)
    terms, columns = call(
        terms_kernel, [shape((16, D), WIDE), shape((D, 16), WIDE)], [VMEM] * 2, flops=4 * 10**9
    )(terms_near, terms_far)
    triple = call(
        triple_kernel,
        shape((3 * width, tokens_here), WIDE),
        [SMEM] + [VMEM] * 5 + [ANYWHERE],
        [
            pltpu.VMEM((3 * width, D), NARROW),
            pltpu.SemaphoreType.DMA,
            pltpu.VMEM((D, tokens_here), NARROW),
        ],
        flops=2 * tokens_here * D * 3 * width, nbytes=5 * 2**20, limit=16,
    )(table, *blocks, columns, attention_weight)
    attended, attention_done = call(
        attention_kernel,
        [shape((tokens_here, width), NARROW), mark],
        [SMEM, VMEM],
        [pltpu.VMEM((width, tokens_here), WIDE)],
        flops=4 * tokens_here * tokens_here * width, trans=4 * tokens_here**2, limit=16,
    )(table, triple)
    split = depth if staged else D
    out_weight, expand_all, reduce_all, tokens, head, bands = call(
        functools.partial(assemble_kernel, [part[:2] for part in parts], split),
        [
            shape((D, D), NARROW),
            shape((D, units), NARROW),
            shape((D, units), NARROW),
            shape((tokens_here, D), NARROW),
            shape((D, NOISE), NARROW),
            shape((IMG_WIDTH, 3 * IMG_WIDTH), WIDE),
        ],
        [SMEM] + [VMEM] * (4 + len(parts)) + [ANYWHERE],
        nbytes=2**23, limit=24,
    )(preview_kernel, *blocks, *(part[2] for part in parts), attention_done)
    across = exchange(attended, "col", 2)
    across = after(across, tokens)
    attended_blocks = (attended, across, exchange(attended, "col", 1), exchange(across, "col", 1))
    if last:
        expand_all, reduce_all = call(
            functools.partial(complete_kernel, [part[:2] for part in last], split),
            [shape((D, units), NARROW)] * 2, [VMEM] * (2 + len(last)), nbytes=2**22, limit=8,
        )(expand_all, reduce_all, *(part[2] for part in last))

    def mlp(offsets, *before):
        outs = [shape((TILE, D), NARROW if offset % 2 else WIDE) for offset in offsets]
        if 0 in offsets:
            outs.append(shape((TILE, D), NARROW))
        outs.append(mark)
        count = len(offsets) * TILE
        return call(
            functools.partial(mlp_kernel, offsets),
            outs,
            [SMEM] + [VMEM] * 9 + [ANYWHERE] * len(before),
            [pltpu.VMEM((count, D), NARROW)] * 2,
            flops=2 * count * D * (D + 2 * units), nbytes=8 * 2**20, trans=count * units, limit=20,
        )(table, *attended_blocks, tokens, terms, out_weight, expand_all, reduce_all, *before)

    far_kept, far_sent, far_done = mlp((2, 3))
    near_sent, _ = mlp((1,), far_done)
    far_sum = (far_kept + exchange(far_sent, "col", 1).astype(WIDE)).astype(NARROW)
    crossed = exchange(far_sum, "col", 2)
    near_kept, residual, _ = mlp((0,), far_sum)
    beside = exchange(near_sent, "col", 1)
    noise = call(
        head_kernel,
        shape((TILE_ROWS, PATCH * IMG_WIDTH), WIDE),
        [SMEM] + [VMEM] * 6,
        flops=4 * TILE * D * IMG_WIDTH, nbytes=2**21, limit=8,
    )(table, near_kept, beside, crossed, residual, terms, head)

    noise_near = pack(noise, exchange(noise, "col", 1))
    img_rows = tiles * IMG_ROWS
    stepped, preview = call(
        step_kernel,
        [shape((img_rows, IMG_WIDTH), NARROW)] * 2,
        [SMEM] * 3 + [VMEM] * 4,
        [pltpu.VMEM((img_rows, IMG_WIDTH), WIDE)] * 2
        + [pltpu.VMEM((img_rows + 16, IMG_WIDTH), WIDE)] * 2,
        flops=12 * img_rows * IMG_WIDTH**2, nbytes=2**19,
    )(table, alpha_now, alpha_next, noise_near, exchange(noise_near, "col", 2), noisy_latent, bands)
    return (stepped, preview)


def solution(mesh):
    return jax.shard_map(
        shards,
        mesh=mesh,
        in_specs=(
            P("row", "col"),
            P("row", None),
            P(),
            P(),
            P(),
            P(),
            P(),
            P("row", None, "col"),
            P(None, None, "col"),
            P("col", None),
            P("row", "col"),
            P("col", "row"),
            P("col", None),
            P(),
        ),
        out_specs=(P("row", None), P("row", None)),
        check_vma=False,
    )
```
